512 devices in a mesh: pts: 64 (over z, x), cen: 8 (over y, core).
Axes of the slice: x: 4, y: 4, z: 16, core: 2. Of those that a mesh axis runs over, the one named last changes fastest.
Arguments:
- points: bfloat16 [65536, 1024], P('pts'), may hold values from -24 to 24
- centroids_t: bfloat16 [1024, 8192], P('pts', 'cen'), may hold values from -0.15 to 0.15
Outputs:
- new_centroids: float32 [1024, 8192], P('pts', 'cen')
- assignments: bfloat16 [65536, 8192], P('pts', 'cen')
The draws below stay inside these ranges and needn't reach their ends.
All inputs are finite; a program needn't handle non-finite values.
Results may differ from the reference program's by a relative error of at most 0.002.
Values may be sent and summed in bfloat16 or wider, within the bound.
A program may use at most 64 MiB of HBM per device.

```python
import math
import jax
import jax.numpy as jnp

D = 1024
PASSES = 3
NPTS = 65536
NCENT = 8192


column_limit = 0.1494140625


def centroid_parts(key):
    keys = jax.random.split(jax.random.fold_in(key, 11), 3)
    signs = jnp.where(jax.random.bernoulli(keys[0], 0.5, (D, NCENT)), 1.0, -1.0)
    unit = signs * jax.random.uniform(keys[1], (D, NCENT), minval=0.8, maxval=1.2) / math.sqrt(D)
    scales = jnp.exp(jax.random.uniform(keys[2], (NCENT,), minval=math.log(0.5), maxval=math.log(2.5)))
    return (unit, scales)


def draw_centroids_t(key, part):
    unit, scales = centroid_parts(key)
    columns = unit * scales[None, :]
    return jnp.clip(columns, -column_limit, column_limit).astype(jnp.bfloat16)


def draw_points(key, part):
    keys = jax.random.split(jax.random.fold_in(key, 23), 2)
    row_ids = jnp.arange(NPTS)
    trend = 0.5 * row_ids.astype(jnp.float32) / NPTS + 0.5 * jax.random.uniform(keys[0], (NPTS,))
    row_scales = jnp.exp(math.log(0.5) + math.log(5.0) * trend)
    values = jnp.clip(jax.random.normal(keys[1], (NPTS, D)), -6.0, 6.0)
    result = row_scales[:, None] * values
    return jnp.clip(result, -24.0, 24.0).astype(jnp.bfloat16)


def setup_inputs(seed: int = 0) -> dict:
    splits = jax.random.split(jax.random.key(seed), 3)
    points = draw_points(jax.random.fold_in(splits[2], 71), 0)
    centroids_t = draw_centroids_t(jax.random.fold_in(splits[2], 71), 0)
    return {"points": points, "centroids_t": centroids_t}


smoothing_scale_factor = 0.8


def reference(points, centroids_t):
    cluster_center_lengths = jnp.sum(jnp.square(centroids_t.astype(jnp.float32)), axis=0)
    pairwise_similarity = jnp.dot(points, centroids_t, preferred_element_type=jnp.float32)
    cluster_score_matrix = (2.0 * pairwise_similarity - cluster_center_lengths[None, :]) / smoothing_scale_factor
    line_highest_entry = jnp.max(cluster_score_matrix, axis=1, keepdims=True)
    weights = jnp.exp(cluster_score_matrix - line_highest_entry)
    transport = weights / jnp.sum(weights, axis=1, keepdims=True)
    for repeat_index in range(PASSES):
        transport = transport / jnp.sum(transport, axis=0, keepdims=True)
        transport = transport / jnp.sum(transport, axis=1, keepdims=True)
    assignments = transport.astype(jnp.bfloat16)
    numerators = jnp.dot(points.T, assignments, preferred_element_type=jnp.float32)
    counts = jnp.sum(assignments, axis=0, dtype=jnp.float32)
    return numerators / counts[None, :], assignments
```

```python
import functools

import jax
import jax.numpy as jnp
from jax import lax
from jax.experimental import pallas as pl
from jax.experimental.pallas import tpu as pltpu
from jax.sharding import PartitionSpec as P

PASSES = 3
MESH = pl.DeviceIdType.MESH
L = 128
F32 = jnp.float32
BF16 = jnp.bfloat16
X_CHIPS = 4
Z_GROUP = 2


def kernel(nx, nz, nc, za, points_ref, cent_ref, newc_ref, assign_ref,
           pts, pts_t, piece, mass, top, assign, own, xsend, xrecv, zsend, zrecv,
           soft, rows, cols_a, cols_b,
           local_sem, gx_send, gx_recv, gz_send, gz_recv, soft_send, soft_recv,
           row_send, row_recv, ca_send, ca_recv, cb_send, cb_recv,
           rx_send, rx_recv, rz_send, rz_recv):
    n_rows, n_d = points_ref.shape
    chunk, n_k = cent_ref.shape
    row_blocks = n_rows // L
    col_tiles = n_k // L
    wide = min(256, n_k)
    zb = nz // za
    na = za * nx
    right_steps = nz // 2
    left_steps = nz - 1 - right_steps

    p = lax.axis_index("pts")
    c = lax.axis_index("cen")
    z = p // nx
    x = p % nx
    ga = (z % za) * nx + x
    gb = z // za

    def cen_peer(o):
        return {"cen": (c + o) % nc}

    def a_peer(o):
        q = (ga + o) % na
        return {"pts": ((z // za) * za + q // nx) * nx + q % nx}

    def b_peer(o):
        return {"pts": (((gb + o) % zb) * za + z % za) * nx + x}

    def x_peer(o):
        return {"pts": z * nx + (x + o) % nx}

    def z_peer(o):
        return {"pts": ((z + nz + o) % nz) * nx + x}

    load = pltpu.make_async_copy(points_ref, pts, local_sem.at[0])
    load.start()

    barrier = pltpu.get_barrier_semaphore()

    def greet(peer, n):
        def body(o, carry):
            pl.semaphore_signal(barrier, inc=1, device_id=peer(o), device_id_type=MESH)
            return carry
        lax.fori_loop(1, n, body, 0)

    greet(cen_peer, nc)
    greet(a_peer, na)
    greet(b_peer, zb)
    pl.semaphore_signal(barrier, inc=1, device_id=z_peer(1), device_id_type=MESH)
    pl.semaphore_signal(barrier, inc=1, device_id=z_peer(-1), device_id_type=MESH)
    pl.semaphore_wait(barrier, (nc - 1) + (na - 1) + (zb - 1) + 2)

    def slab(first, n):
        return piece.at[pl.ds(pl.multiple_of(first * chunk, chunk), n * chunk), :]

    piece[pl.ds(pl.multiple_of(p * chunk, chunk), chunk), :] = cent_ref[...]

    def gx(o):
        return pltpu.make_async_remote_copy(
            src_ref=slab(p, 1), dst_ref=slab(p, 1), send_sem=gx_send.at[o], recv_sem=gx_recv.at[o],
            device_id=x_peer(o), device_id_type=MESH)

    def gx_start(o, carry):
        gx(o).start()
        return carry

    def gx_wait(o, carry):
        gx(o).wait()
        return carry

    lax.fori_loop(1, nx, gx_start, 0)
    lax.fori_loop(1, nx, gx_wait, 0)

    def gz(side, s):
        block = (z - s + nz) % nz if side == 0 else (z + s) % nz
        return pltpu.make_async_remote_copy(
            src_ref=slab(block * nx, nx), dst_ref=slab(block * nx, nx),
            send_sem=gz_send.at[side, s], recv_sem=gz_recv.at[side, s],
            device_id=z_peer(1 if side == 0 else -1), device_id_type=MESH)

    d_blocks = n_d // L
    per = L // chunk

    def turn(b):
        block = pts[:, pl.ds(pl.multiple_of(b * L, L), L)].astype(F32)
        flipped = block.T.astype(BF16)
        for g in range(per):
            place = (g % nx) * nz + b * (per // nx) + g // nx
            pts_t[pl.ds(pl.multiple_of(place * chunk, chunk), chunk), :] = flipped[g * chunk:(g + 1) * chunk, :]

    gz(0, 0).start()
    gz(1, 0).start()
    load.wait()

    def ring(s, carry):
        gz(0, s).wait_recv()
        gz(0, s + 1).start()
        gz(1, s).wait_recv()

        @pl.when(s + 1 < left_steps)
        def _():
            gz(1, s + 1).start()
        return carry

    def turn_step(b, carry):
        turn(b)
        return carry

    lax.fori_loop(0, left_steps, ring, 0)
    lax.fori_loop(0, d_blocks, turn_step, 0)
    gz(0, right_steps - 1).wait_recv()

    def gz_drain(s, carry):
        gz(0, s).wait_send()

        @pl.when(s < left_steps)
        def _():
            gz(1, s).wait_send()
        return carry

    lax.fori_loop(0, right_steps, gz_drain, 0)

    top[...] = jnp.full(top.shape, -jnp.inf, F32)

    def logits(t, carry):
        where = pl.ds(pl.multiple_of(t * wide, wide), wide)
        part = piece[:, where]
        long = part.astype(F32)
        norms = jnp.sum(long * long, axis=0, keepdims=True)
        dots = jnp.dot(pts[...], part, preferred_element_type=F32)
        score = (2.0 * dots - norms) * 1.25
        mass[:, where] = score
        best = score[:, :L]
        for i in range(1, wide // L):
            best = jnp.maximum(best, score[:, i * L:(i + 1) * L])
        top[...] = jnp.maximum(top[...], best)
        return carry

    lax.fori_loop(0, n_k // wide, logits, 0)

    def swap(buf, slot, n, me, peer, send, recv):
        def copy(o):
            return pltpu.make_async_remote_copy(
                src_ref=buf.at[me], dst_ref=buf.at[me], send_sem=send.at[slot, o],
                recv_sem=recv.at[slot, o], device_id=peer(o), device_id_type=MESH)

        def start(o, carry):
            copy(o).start()
            return carry

        def wait(o, carry):
            copy(o).wait()
            return carry

        return (lambda: lax.fori_loop(1, n, start, 0)), (lambda: lax.fori_loop(1, n, wait, 0))

    def total(buf, n):
        out = buf[0]
        for i in range(1, n):
            out = out + buf[i]
        return out

    def row_block(j):
        return pl.ds(pl.multiple_of(j * L, L), L)

    def weigh(j, carry):
        block = top[row_block(j), :]
        peak = jnp.max(block, axis=1, keepdims=True)
        soft[c, pl.ds(j, 1), :] = jnp.max(block.T, axis=0, keepdims=True)
        acc = jnp.zeros((L, L), F32)
        for t in range(col_tiles):
            w = jnp.exp(mass[row_block(j), t * L:(t + 1) * L] - peak)
            mass[row_block(j), t * L:(t + 1) * L] = w
            acc = acc + w
        soft[c, pl.ds(row_blocks + j, 1), :] = jnp.sum(acc.T, axis=0, keepdims=True)
        return carry

    lax.fori_loop(0, row_blocks, weigh, 0)
    start, wait = swap(soft, 0, nc, c, cen_peer, soft_send, soft_recv)
    start()
    wait()
    peaks = soft[0, :row_blocks]
    for i in range(1, nc):
        peaks = jnp.maximum(peaks, soft[i, :row_blocks])
    sums = jnp.zeros_like(peaks)
    for i in range(nc):
        sums = sums + soft[i, row_blocks:] * jnp.exp(soft[i, :row_blocks] - peaks)
    scale_rows = jnp.exp(soft[c, :row_blocks] - peaks) / sums

    def spread(scales, j):
        return jnp.broadcast_to(scales[j:j + 1, :], (L, L)).T

    def add_down(v):
        return jnp.sum(v, axis=0, keepdims=True)

    def reduce_cols(slot):
        start_a, wait_a = swap(cols_a.at[slot], slot, na, ga, a_peer, ca_send, ca_recv)
        start_b, wait_b = swap(cols_b.at[slot], slot, zb, gb, b_peer, cb_send, cb_recv)

        def middle():
            wait_a()
            cols_b[slot, gb] = total(cols_a.at[slot], na)
            start_b()

        def last():
            wait_b()
            return total(cols_b.at[slot], zb)

        return start_a, middle, last

    for turn_no in range(PASSES):
        acc = [jnp.zeros((1, L), F32) for _ in range(col_tiles)]
        for j in range(row_blocks):
            scale = spread(scale_rows, j)
            for t in range(col_tiles):
                m = mass[j * L:(j + 1) * L, t * L:(t + 1) * L] * scale
                mass[j * L:(j + 1) * L, t * L:(t + 1) * L] = m
                acc[t] = acc[t] + add_down(m)
        for t in range(col_tiles):
            cols_a[turn_no, ga, t:t + 1, :] = acc[t]
        first, middle, last = reduce_cols(turn_no)
        first()
        middle()
        scale_cols = 1.0 / last()
        for j in range(row_blocks):
            acc_r = jnp.zeros((L, L), F32)
            for t in range(col_tiles):
                m = mass[j * L:(j + 1) * L, t * L:(t + 1) * L] * scale_cols[t:t + 1, :]
                mass[j * L:(j + 1) * L, t * L:(t + 1) * L] = m
                acc_r = acc_r + m
            rows[turn_no, c, j:j + 1, :] = add_down(acc_r.T)
        start, wait = swap(rows.at[turn_no], turn_no, nc, c, cen_peer, row_send, row_recv)
        start()
        wait()
        scale_rows = 1.0 / total(rows.at[turn_no], nc)

    acc = [jnp.zeros((1, L), F32) for _ in range(col_tiles)]
    for j in range(row_blocks):
        scale = spread(scale_rows, j)
        for t in range(col_tiles):
            m = (mass[j * L:(j + 1) * L, t * L:(t + 1) * L] * scale).astype(BF16)
            assign[j * L:(j + 1) * L, t * L:(t + 1) * L] = m
            acc[t] = acc[t] + add_down(m.astype(F32))
    store = pltpu.make_async_copy(assign, assign_ref, local_sem.at[1])
    store.start()
    for t in range(col_tiles):
        cols_a[PASSES, ga, t:t + 1, :] = acc[t]
    first, middle, last = reduce_cols(PASSES)
    first()

    half = n_d // nx

    def rx(o):
        return pltpu.make_async_remote_copy(
            src_ref=xsend.at[o - 1], dst_ref=xrecv.at[o - 1], send_sem=rx_send.at[o], recv_sem=rx_recv.at[o],
            device_id=x_peer(o), device_id_type=MESH)

    order = sorted(range(1, nx), key=lambda o: -min(o, nx - o)) + [0]
    for o in order:
        to = (x + o) % nx
        lhs_rows = pl.ds(pl.multiple_of(to * half, half), half)

        def product(t, carry):
            where = pl.ds(pl.multiple_of(t * wide, wide), wide)
            part = jnp.dot(pts_t[lhs_rows, :], assign[:, where], preferred_element_type=F32)
            if o:
                xsend[o - 1, :, where] = part.astype(BF16)
            else:
                own[:, where] = part
            return carry

        lax.fori_loop(0, n_k // wide, product, 0)
        if o:
            rx(o).start()
    middle()

    for o in range(1, nx):
        rx(o).wait_recv()

    def gather_up(i, carry):
        here = pl.ds(pl.multiple_of(i * chunk, chunk), chunk)
        v = own[here, :]
        for o in range(1, nx):
            v = v + xrecv[o - 1, here, :].astype(F32)
        own[here, :] = v
        return carry

    lax.fori_loop(0, nz, gather_up, 0)

    def share(b):
        return own[pl.ds(pl.multiple_of(b * chunk, chunk), chunk), :]

    def rz(side, s):
        return pltpu.make_async_remote_copy(
            src_ref=zsend.at[side, s], dst_ref=zrecv.at[side, s],
            send_sem=rz_send.at[side, s], recv_sem=rz_recv.at[side, s],
            device_id=z_peer(1 if side == 0 else -1), device_id_type=MESH)

    zsend[0, 0] = share((z + right_steps) % nz)
    rz(0, 0).start()
    zsend[1, 0] = share((z + nz - left_steps) % nz)
    rz(1, 0).start()

    def ring_sum(s, carry):
        rz(0, s - 1).wait_recv()
        zsend[0, s] = zrecv[0, s - 1] + share((z + right_steps - s) % nz)
        rz(0, s).start()
        rz(1, s - 1).wait_recv()

        @pl.when(s < left_steps)
        def _():
            zsend[1, s] = zrecv[1, s - 1] + share((z + nz - left_steps + s) % nz)
            rz(1, s).start()
        return carry

    lax.fori_loop(1, right_steps, ring_sum, 0)
    counts = last()
    rz(0, right_steps - 1).wait_recv()
    numer = share(z) + zrecv[0, right_steps - 1] + zrecv[1, left_steps - 1]
    for t in range(col_tiles):
        newc_ref[:, t * L:(t + 1) * L] = numer[:, t * L:(t + 1) * L] / counts[t:t + 1, :]

    def rz_drain(s, carry):
        rz(0, s).wait_send()

        @pl.when(s < left_steps)
        def _():
            rz(1, s).wait_send()
        return carry

    lax.fori_loop(0, right_steps, rz_drain, 0)
    for o in range(1, nx):
        rx(o).wait_send()
    store.wait()


def on_device(nx, nz, nc, za, points, centroids_t):
    n_rows, n_d = points.shape
    chunk, n_k = centroids_t.shape
    na, zb = za * nx, nz // za
    rb, ct = n_rows // L, n_k // L
    assert nz // 2 == nz - 1 - nz // 2 + 1
    right = nz // 2
    vmem = pltpu.VMEM
    dma = pltpu.SemaphoreType.DMA
    return pl.pallas_call(
        functools.partial(kernel, nx, nz, nc, za),
        out_shape=(
            jax.ShapeDtypeStruct((chunk, n_k), F32),
            jax.ShapeDtypeStruct((n_rows, n_k), BF16),
        ),
        in_specs=[pl.BlockSpec(memory_space=pl.ANY), pl.BlockSpec(memory_space=vmem)],
        out_specs=(pl.BlockSpec(memory_space=vmem), pl.BlockSpec(memory_space=pl.ANY)),
        scratch_shapes=[
            vmem((n_rows, n_d), BF16),
            vmem((n_d, n_rows), BF16),
            vmem((n_d, n_k), BF16),
            vmem((n_rows, n_k), F32),
            vmem((n_rows, L), F32),
            vmem((n_rows, n_k), BF16),
            vmem((n_d // nx, n_k), F32),
            vmem((nx - 1, n_d // nx, n_k), BF16),
            vmem((nx - 1, n_d // nx, n_k), BF16),
            vmem((2, right, chunk, n_k), F32),
            vmem((2, right, chunk, n_k), F32),
            vmem((nc, 2 * rb, L), F32),
            vmem((PASSES, nc, rb, L), F32),
            vmem((PASSES + 1, na, ct, L), F32),
            vmem((PASSES + 1, zb, ct, L), F32),
            dma((2,)),
            dma((nx,)), dma((nx,)),
            dma((2, right)), dma((2, right)),
            dma((1, nc)), dma((1, nc)),
            dma((PASSES, nc)), dma((PASSES, nc)),
            dma((PASSES + 1, na)), dma((PASSES + 1, na)),
            dma((PASSES + 1, zb)), dma((PASSES + 1, zb)),
            dma((nx,)), dma((nx,)),
            dma((2, right)), dma((2, right)),
        ],
        compiler_params=pltpu.CompilerParams(
            collective_id=0, has_side_effects=True, vmem_limit_bytes=50 * 1024 * 1024
        ),
    )(points, centroids_t)


def solution(mesh, nx=X_CHIPS, za=Z_GROUP):
    nz = mesh.shape["pts"] // nx
    return jax.shard_map(
        functools.partial(on_device, nx, nz, mesh.shape["cen"], za),
        mesh=mesh,
        in_specs=(P("pts", None), P("pts", "cen")),
        out_specs=(P("pts", "cen"), P("pts", "cen")),
        check_vma=False,
    )
```

```python
import functools

import jax
import jax.numpy as jnp
from jax import lax
from jax.experimental import pallas as pl
from jax.experimental.pallas import tpu as pltpu
from jax.sharding import PartitionSpec as P

PASSES = 3
MESH = pl.DeviceIdType.MESH
L = 128
F32 = jnp.float32
BF16 = jnp.bfloat16
X_CHIPS = 4
Z_GROUP = 2


def kernel(nx, nz, nc, za, points_ref, cent_ref, newc_ref, assign_ref,
           pts, pts_t, piece, mass, norms, top, assign, own, xsend, xrecv, zsend, zrecv,
           soft, rows, cols_a, cols_b,
           local_sem, gx_send, gx_recv, gz_send, gz_recv, soft_send, soft_recv,
           row_send, row_recv, ca_send, ca_recv, cb_send, cb_recv,
           rx_send, rx_recv, rz_send, rz_recv):
    n_rows, n_d = points_ref.shape
    chunk, n_k = cent_ref.shape
    row_blocks = n_rows // L
    col_tiles = n_k // L
    wide = min(256, n_k)
    zb = nz // za
    na = za * nx
    right_steps = nz // 2
    left_steps = nz - 1 - right_steps

    p = lax.axis_index("pts")
    c = lax.axis_index("cen")
    z = p // nx
    x = p % nx
    ga = (z % za) * nx + x
    gb = z // za

    def cen_peer(o):
        return {"cen": (c + o) % nc}

    def a_peer(o):
        q = (ga + o) % na
        return {"pts": ((z // za) * za + q // nx) * nx + q % nx}

    def b_peer(o):
        return {"pts": (((gb + o) % zb) * za + z % za) * nx + x}

    def x_peer(o):
        return {"pts": z * nx + (x + o) % nx}

    def z_peer(o):
        return {"pts": ((z + nz + o) % nz) * nx + x}

    load = pltpu.make_async_copy(points_ref, pts, local_sem.at[0])
    load.start()

    barrier = pltpu.get_barrier_semaphore()

    def greet(peer, n):
        def body(o, carry):
            pl.semaphore_signal(barrier, inc=1, device_id=peer(o), device_id_type=MESH)
            return carry
        lax.fori_loop(1, n, body, 0)

    greet(cen_peer, nc)
    greet(x_peer, nx)
    pl.semaphore_signal(barrier, inc=1, device_id=z_peer(1), device_id_type=MESH)
    pl.semaphore_signal(barrier, inc=1, device_id=z_peer(-1), device_id_type=MESH)
    pl.semaphore_wait(barrier, (nc - 1) + (nx - 1) + 2)

    def slab(first, n):
        return piece.at[pl.ds(pl.multiple_of(first * chunk, chunk), n * chunk), :]

    piece[pl.ds(pl.multiple_of(p * chunk, chunk), chunk), :] = cent_ref[...]

    def gx(o):
        return pltpu.make_async_remote_copy(
            src_ref=slab(p, 1), dst_ref=slab(p, 1), send_sem=gx_send.at[o], recv_sem=gx_recv.at[o],
            device_id=x_peer(o), device_id_type=MESH)

    for o in range(1, nx):
        gx(o).start()

    def gz(side, s, o):
        block = (z - s + nz) % nz if side == 0 else (z + s) % nz
        part = slab(block * nx + (x - o + nx) % nx, 1)
        return pltpu.make_async_remote_copy(
            src_ref=part, dst_ref=part,
            send_sem=gz_send.at[side, s, o], recv_sem=gz_recv.at[side, s, o],
            device_id=z_peer(1 if side == 0 else -1), device_id_type=MESH)

    near = sorted(range(nx), key=lambda o: min(o, nx - o))
    for o in near:
        if o:
            gx(o).wait_recv()
        gz(0, 0, o).start()
        gz(1, 0, o).start()

    d_blocks = n_d // L
    per = L // chunk

    def turn(b):
        block = pts[:, pl.ds(pl.multiple_of(b * L, L), L)].astype(F32)
        flipped = block.T.astype(BF16)
        for g in range(per):
            place = (g % nx) * nz + b * (per // nx) + g // nx
            pts_t[pl.ds(pl.multiple_of(place * chunk, chunk), chunk), :] = flipped[g * chunk:(g + 1) * chunk, :]

    load.wait()
    for b in range(left_steps, d_blocks):
        turn(b)

    def ring(s, carry):
        for o in near:
            gz(0, s, o).wait_recv()
            gz(0, s + 1, o).start()
            gz(1, s, o).wait_recv()

            @pl.when(s + 1 < left_steps)
            def _():
                gz(1, s + 1, o).start()

        @pl.when(s < d_blocks)
        def _():
            turn(s)
        return carry

    quarter = n_d // 4
    mine = z // (nz // 4)

    def depth(g):
        return pl.ds(pl.multiple_of(g * quarter, quarter), quarter)

    def dots_of(g, where):
        part = piece[depth(g), where]
        long = part.astype(F32)
        dots = jnp.dot(pts[:, depth(g)], part, preferred_element_type=F32)
        return dots, jnp.sum(long * long, axis=0, keepdims=True)

    def first_dots(t, carry):
        where = pl.ds(pl.multiple_of(t * wide, wide), wide)
        dots, squares = dots_of(mine, where)
        mass[:, where] = dots
        norms[:, where] = squares
        return carry

    def more_dots(g):
        def body(t, carry):
            where = pl.ds(pl.multiple_of(t * wide, wide), wide)
            dots, squares = dots_of(g, where)
            mass[:, where] += dots
            norms[:, where] += squares
            return carry
        return body

    tiles = n_k // wide
    lax.fori_loop(0, nz // 4, ring, 0)
    lax.fori_loop(0, tiles, first_dots, 0)
    lax.fori_loop(nz // 4, left_steps, ring, 0)
    lax.fori_loop(0, tiles, more_dots((mine + 1) % 4), 0)
    lax.fori_loop(0, tiles, more_dots((mine + 3) % 4), 0)
    for o in near:
        gz(0, right_steps - 1, o).wait_recv()
    top[...] = jnp.full(top.shape, -jnp.inf, F32)

    def logits(t, carry):
        where = pl.ds(pl.multiple_of(t * wide, wide), wide)
        dots, squares = dots_of((mine + 2) % 4, where)
        score = (2.0 * (mass[:, where] + dots) - (norms[:, where] + squares)) * 1.25
        mass[:, where] = score
        best = score[:, :L]
        for i in range(1, wide // L):
            best = jnp.maximum(best, score[:, i * L:(i + 1) * L])
        top[...] = jnp.maximum(top[...], best)
        return carry

    lax.fori_loop(0, tiles, logits, 0)

    def gz_drain(s, carry):
        for o in range(nx):
            gz(0, s, o).wait_send()

            @pl.when(s < left_steps)
            def _():
                gz(1, s, o).wait_send()
        return carry

    lax.fori_loop(0, right_steps, gz_drain, 0)
    for o in range(1, nx):
        gx(o).wait_send()

    def swap(buf, slot, n, me, peer, send, recv):
        def copy(o):
            return pltpu.make_async_remote_copy(
                src_ref=buf.at[me], dst_ref=buf.at[me], send_sem=send.at[slot, o],
                recv_sem=recv.at[slot, o], device_id=peer(o), device_id_type=MESH)

        def start(o, carry):
            copy(o).start()
            return carry

        def wait(o, carry):
            copy(o).wait()
            return carry

        return (lambda: lax.fori_loop(1, n, start, 0)), (lambda: lax.fori_loop(1, n, wait, 0))

    def total(buf, n):
        out = buf[0]
        for i in range(1, n):
            out = out + buf[i]
        return out

    def row_block(j):
        return pl.ds(pl.multiple_of(j * L, L), L)

    def weigh(j, carry):
        block = top[row_block(j), :]
        peak = jnp.max(block, axis=1, keepdims=True)
        soft[c, pl.ds(j, 1), :] = jnp.max(block.T, axis=0, keepdims=True)
        acc = jnp.zeros((L, L), F32)
        for t in range(col_tiles):
            w = jnp.exp(mass[row_block(j), t * L:(t + 1) * L] - peak)
            mass[row_block(j), t * L:(t + 1) * L] = w
            acc = acc + w
        soft[c, pl.ds(row_blocks + j, 1), :] = jnp.sum(acc.T, axis=0, keepdims=True)
        return carry

    lax.fori_loop(0, row_blocks, weigh, 0)
    start, wait = swap(soft, 0, nc, c, cen_peer, soft_send, soft_recv)
    start()
    wait()
    peaks = soft[0, :row_blocks]
    for i in range(1, nc):
        peaks = jnp.maximum(peaks, soft[i, :row_blocks])
    sums = jnp.zeros_like(peaks)
    for i in range(nc):
        sums = sums + soft[i, row_blocks:] * jnp.exp(soft[i, :row_blocks] - peaks)
    scale_rows = jnp.exp(soft[c, :row_blocks] - peaks) / sums

    def spread(scales, j):
        return jnp.broadcast_to(scales[j:j + 1, :], (L, L)).T

    def add_down(v):
        return jnp.sum(v, axis=0, keepdims=True)

    def reduce_cols(slot):
        start_a, wait_a = swap(cols_a.at[slot], slot, na, ga, a_peer, ca_send, ca_recv)
        start_b, wait_b = swap(cols_b.at[slot], slot, zb, gb, b_peer, cb_send, cb_recv)

        def middle():
            wait_a()
            cols_b[slot, gb] = total(cols_a.at[slot], na)
            start_b()

        def last():
            wait_b()
            return total(cols_b.at[slot], zb)

        return start_a, middle, last

    for turn_no in range(PASSES):
        acc = [jnp.zeros((1, L), F32) for _ in range(col_tiles)]
        for j in range(row_blocks):
            scale = spread(scale_rows, j)
            for t in range(col_tiles):
                m = mass[j * L:(j + 1) * L, t * L:(t + 1) * L] * scale
                mass[j * L:(j + 1) * L, t * L:(t + 1) * L] = m
                acc[t] = acc[t] + add_down(m)
        for t in range(col_tiles):
            cols_a[turn_no, ga, t:t + 1, :] = acc[t]
        first, middle, last = reduce_cols(turn_no)
        first()
        middle()
        scale_cols = 1.0 / last()
        for j in range(row_blocks):
            acc_r = jnp.zeros((L, L), F32)
            for t in range(col_tiles):
                m = mass[j * L:(j + 1) * L, t * L:(t + 1) * L] * scale_cols[t:t + 1, :]
                mass[j * L:(j + 1) * L, t * L:(t + 1) * L] = m
                acc_r = acc_r + m
            rows[turn_no, c, j:j + 1, :] = add_down(acc_r.T)
        start, wait = swap(rows.at[turn_no], turn_no, nc, c, cen_peer, row_send, row_recv)
        start()
        wait()
        scale_rows = 1.0 / total(rows.at[turn_no], nc)

    acc = [jnp.zeros((1, L), F32) for _ in range(col_tiles)]
    for j in range(row_blocks):
        scale = spread(scale_rows, j)
        for t in range(col_tiles):
            m = (mass[j * L:(j + 1) * L, t * L:(t + 1) * L] * scale).astype(BF16)
            assign[j * L:(j + 1) * L, t * L:(t + 1) * L] = m
            acc[t] = acc[t] + add_down(m.astype(F32))
    store = pltpu.make_async_copy(assign, assign_ref, local_sem.at[1])
    store.start()
    for t in range(col_tiles):
        cols_a[PASSES, ga, t:t + 1, :] = acc[t]
    first, middle, last = reduce_cols(PASSES)
    first()

    half = n_d // nx

    def rx(o):
        return pltpu.make_async_remote_copy(
            src_ref=xsend.at[o - 1], dst_ref=xrecv.at[o - 1], send_sem=rx_send.at[o], recv_sem=rx_recv.at[o],
            device_id=x_peer(o), device_id_type=MESH)

    order = sorted(range(1, nx), key=lambda o: -min(o, nx - o)) + [0]
    for o in order:
        to = (x + o) % nx
        lhs_rows = pl.ds(pl.multiple_of(to * half, half), half)

        def product(t, carry):
            where = pl.ds(pl.multiple_of(t * wide, wide), wide)
            part = jnp.dot(pts_t[lhs_rows, :], assign[:, where], preferred_element_type=F32)
            if o:
                xsend[o - 1, :, where] = part.astype(BF16)
            else:
                own[:, where] = part
            return carry

        lax.fori_loop(0, n_k // wide, product, 0)
        if o:
            rx(o).start()
    middle()

    for o in range(1, nx):
        rx(o).wait_recv()

    def gather_up(i, carry):
        here = pl.ds(pl.multiple_of(i * chunk, chunk), chunk)
        v = own[here, :]
        for o in range(1, nx):
            v = v + xrecv[o - 1, here, :].astype(F32)
        own[here, :] = v
        return carry

    lax.fori_loop(0, nz, gather_up, 0)

    def share(b):
        return own[pl.ds(pl.multiple_of(b * chunk, chunk), chunk), :]

    def rz(side, s):
        return pltpu.make_async_remote_copy(
            src_ref=zsend.at[side, s], dst_ref=zrecv.at[side, s],
            send_sem=rz_send.at[side, s], recv_sem=rz_recv.at[side, s],
            device_id=z_peer(1 if side == 0 else -1), device_id_type=MESH)

    zsend[0, 0] = share((z + right_steps) % nz)
    rz(0, 0).start()
    zsend[1, 0] = share((z + nz - left_steps) % nz)
    rz(1, 0).start()

    def ring_sum(s, carry):
        rz(0, s - 1).wait_recv()
        zsend[0, s] = zrecv[0, s - 1] + share((z + right_steps - s) % nz)
        rz(0, s).start()
        rz(1, s - 1).wait_recv()

        @pl.when(s < left_steps)
        def _():
            zsend[1, s] = zrecv[1, s - 1] + share((z + nz - left_steps + s) % nz)
            rz(1, s).start()
        return carry

    lax.fori_loop(1, right_steps, ring_sum, 0)
    counts = last()
    rz(0, right_steps - 1).wait_recv()
    numer = share(z) + zrecv[0, right_steps - 1] + zrecv[1, left_steps - 1]
    for t in range(col_tiles):
        newc_ref[:, t * L:(t + 1) * L] = numer[:, t * L:(t + 1) * L] / counts[t:t + 1, :]

    def rz_drain(s, carry):
        rz(0, s).wait_send()

        @pl.when(s < left_steps)
        def _():
            rz(1, s).wait_send()
        return carry

    lax.fori_loop(0, right_steps, rz_drain, 0)
    for o in range(1, nx):
        rx(o).wait_send()
    store.wait()


def on_device(nx, nz, nc, za, points, centroids_t):
    n_rows, n_d = points.shape
    chunk, n_k = centroids_t.shape
    na, zb = za * nx, nz // za
    rb, ct = n_rows // L, n_k // L
    assert nz // 2 == nz - 1 - nz // 2 + 1
    right = nz // 2
    vmem = pltpu.VMEM
    dma = pltpu.SemaphoreType.DMA
    return pl.pallas_call(
        functools.partial(kernel, nx, nz, nc, za),
        out_shape=(
            jax.ShapeDtypeStruct((chunk, n_k), F32),
            jax.ShapeDtypeStruct((n_rows, n_k), BF16),
        ),
        in_specs=[pl.BlockSpec(memory_space=pl.ANY), pl.BlockSpec(memory_space=vmem)],
        out_specs=(pl.BlockSpec(memory_space=vmem), pl.BlockSpec(memory_space=pl.ANY)),
        scratch_shapes=[
            vmem((n_rows, n_d), BF16),
            vmem((n_d, n_rows), BF16),
            vmem((n_d, n_k), BF16),
            vmem((n_rows, n_k), F32),
            vmem((1, n_k), F32),
            vmem((n_rows, L), F32),
            vmem((n_rows, n_k), BF16),
            vmem((n_d // nx, n_k), F32),
            vmem((nx - 1, n_d // nx, n_k), BF16),
            vmem((nx - 1, n_d // nx, n_k), BF16),
            vmem((2, right, chunk, n_k), F32),
            vmem((2, right, chunk, n_k), F32),
            vmem((nc, 2 * rb, L), F32),
            vmem((PASSES, nc, rb, L), F32),
            vmem((PASSES + 1, na, ct, L), F32),
            vmem((PASSES + 1, zb, ct, L), F32),
            dma((2,)),
            dma((nx,)), dma((nx,)),
            dma((2, right, nx)), dma((2, right, nx)),
            dma((1, nc)), dma((1, nc)),
            dma((PASSES, nc)), dma((PASSES, nc)),
            dma((PASSES + 1, na)), dma((PASSES + 1, na)),
            dma((PASSES + 1, zb)), dma((PASSES + 1, zb)),
            dma((nx,)), dma((nx,)),
            dma((2, right)), dma((2, right)),
        ],
        compiler_params=pltpu.CompilerParams(
            collective_id=0, has_side_effects=True, vmem_limit_bytes=50 * 1024 * 1024
        ),
    )(points, centroids_t)


def solution(mesh, nx=X_CHIPS, za=Z_GROUP):
    nz = mesh.shape["pts"] // nx
    return jax.shard_map(
        functools.partial(on_device, nx, nz, mesh.shape["cen"], za),
        mesh=mesh,
        in_specs=(P("pts", None), P("pts", "cen")),
        out_specs=(P("pts", "cen"), P("pts", "cen")),
        check_vma=False,
    )
```

```python
import functools

import jax
import jax.numpy as jnp
from jax import lax
from jax.experimental import pallas as pl
from jax.experimental.pallas import tpu as pltpu
from jax.sharding import PartitionSpec as P

PASSES = 3
MESH = pl.DeviceIdType.MESH
L = 128
F32 = jnp.float32
BF16 = jnp.bfloat16
X_CHIPS = 4
Z_GROUP = 2
VIA = {1: 1, -1: -1, 2: -1, 4: 1, 5: -1, 7: 1, 8: 2, -2: 1, -4: -1, -5: 1, -7: -1}
FEEDS = {3: (4, 2), 6: (7, 5, 8), -3: (-4, -2), -6: (-7, -5)}
FAR = (6, -6, 3, -3)
GREET_Z = (1, -1, 2, -2, 3, -3, 6, -6)
PARTS = ((5, 4), (-7, 3), (2, 3), (-4, 3), (-1, 3))


def kernel(nx, nz, nc, za, points_ref, cent_ref, newc_ref, assign_ref,
           pts, pts_t, piece, mass, norms, top, assign, own, prod, xsend, xrecv, zrecv,
           soft, rows, cols_a, cols_b,
           local_sem, gx_send, gx_recv, gz_send, gz_recv, soft_send, soft_recv,
           row_send, row_recv, ca_send, ca_recv, cb_send, cb_recv,
           rx_send, rx_recv, rz_send, rz_recv):
    n_rows, n_d = points_ref.shape
    chunk, n_k = cent_ref.shape
    row_blocks = n_rows // L
    col_tiles = n_k // L
    wide = min(256, n_k)
    zb = nz // za
    na = za * nx

    p = lax.axis_index("pts")
    c = lax.axis_index("cen")
    z = p // nx
    x = p % nx
    ga = (z % za) * nx + x
    gb = z // za

    def cen_peer(o):
        return {"cen": (c + o) % nc}

    def a_peer(o):
        q = (ga + o) % na
        return {"pts": ((z // za) * za + q // nx) * nx + q % nx}

    def b_peer(o):
        return {"pts": (((gb + o) % zb) * za + z % za) * nx + x}

    def x_peer(o):
        return {"pts": z * nx + (x + o) % nx}

    def z_peer(o):
        return {"pts": ((z + nz + o) % nz) * nx + x}

    load = pltpu.make_async_copy(points_ref, pts, local_sem.at[0])
    load.start()

    barrier = pltpu.get_barrier_semaphore()

    def greet(peer, n):
        def body(o, carry):
            pl.semaphore_signal(barrier, inc=1, device_id=peer(o), device_id_type=MESH)
            return carry
        lax.fori_loop(1, n, body, 0)

    greet(cen_peer, nc)
    greet(x_peer, nx)
    for e in GREET_Z:
        pl.semaphore_signal(barrier, inc=1, device_id=z_peer(e), device_id_type=MESH)
    pl.semaphore_wait(barrier, (nc - 1) + (nx - 1) + len(GREET_Z))

    def slab(e, side):
        first = ((z + nz + e) % nz) * nx + (x + nx + side) % nx
        return piece.at[pl.ds(pl.multiple_of(first * chunk, chunk), chunk), :]

    piece[pl.ds(pl.multiple_of(p * chunk, chunk), chunk), :] = cent_ref[...]

    def gz(e, root):
        at = root - e + 7
        at = at + nz if at < 0 else at - nz if at >= nz else at
        part = slab(root, 0)
        return pltpu.make_async_remote_copy(
            src_ref=part, dst_ref=part, send_sem=gz_send.at[at], recv_sem=gz_recv.at[at],
            device_id=z_peer(e), device_id_type=MESH)

    def gz_got(e):
        part = slab(e, 0)
        return pltpu.make_async_remote_copy(
            src_ref=part, dst_ref=part, send_sem=gz_send.at[e + 7], recv_sem=gz_recv.at[e + 7],
            device_id=z_peer(1), device_id_type=MESH)

    def gx(e, frm, side):
        part = slab(e, frm)
        lane = 0 if frm == 0 and side == 1 else 1 if frm == 0 else 2
        return pltpu.make_async_remote_copy(
            src_ref=part, dst_ref=part, send_sem=gx_send.at[e + 7, lane], recv_sem=gx_recv.at[e + 7, lane],
            device_id=x_peer(nx + side), device_id_type=MESH)

    def gx_got(e, lane):
        part = slab(e, (-1, 1, 2)[lane])
        return pltpu.make_async_remote_copy(
            src_ref=part, dst_ref=part, send_sem=gx_send.at[e + 7, lane], recv_sem=gx_recv.at[e + 7, lane],
            device_id=x_peer(1), device_id_type=MESH)

    sent_z = []
    sent_x = []

    def go_z(e, root):
        gz(e, root).start()
        sent_z.append((e, root))

    def go_x(e, frm, side):
        gx(e, frm, side).start()
        sent_x.append((e, frm, side))

    def x_near(e):
        go_x(e, 0, 1)
        go_x(e, 0, -1)

    def x_on(e):
        gx_got(e, 0).wait_recv()
        gx_got(e, 1).wait_recv()
        if e % 2 == 0:
            go_x(e, -1, 1)
        else:
            go_x(e, 1, -1)

    d_blocks = n_d // L

    def turn(b):
        block = pts[:, pl.ds(pl.multiple_of(b * L, L), L)].astype(F32)
        pts_t[pl.ds(pl.multiple_of(b * L, L), L), :] = block.T.astype(BF16)

    def turns(first, last):
        def body(b, carry):
            turn(b)
            return carry
        lax.fori_loop(first, last, body, 0)

    for e in FAR + (1, -1):
        go_z(e, 0)
    x_near(0)
    load.wait()
    turns(0, d_blocks // 2)
    for e in (1, -1):
        gz_got(e).wait_recv()
        x_near(e)
    for e in (3, -3):
        gz_got(e).wait_recv()
        go_z(1, e)
        go_z(-1, e)
        x_near(e)
    x_on(0)
    for e in (6, -6):
        gz_got(e).wait_recv()
        go_z(1, e)
        go_z(-1, e)
        if e == -6:
            go_z(2, e)
        x_near(e)
    for e in (1, -1, 3, -3):
        x_on(e)
    for e in (2, -2, 4, -4):
        gz_got(e).wait_recv()
        x_near(e)
    x_on(6)
    x_on(-6)
    for e in (5, -5, 7, -7, 8):
        gz_got(e).wait_recv()
        x_near(e)
    turns(d_blocks // 2, d_blocks)
    ahead = 3 * nx * chunk
    pts_t[n_d:n_d + ahead, :] = pts_t[:ahead, :]
    for e in (2, -2, 4, -4, 5, -5, 7, -7, 8):
        x_on(e)

    quarter = n_d // 4
    mine = z // (nz // 4)

    def depth(g):
        return pl.ds(pl.multiple_of(g * quarter, quarter), quarter)

    def dots_of(g, where):
        part = piece[depth(g), where]
        long = part.astype(F32)
        dots = jnp.dot(pts[:, depth(g)], part, preferred_element_type=F32)
        return dots, jnp.sum(long * long, axis=0, keepdims=True)

    def first_dots(t, carry):
        where = pl.ds(pl.multiple_of(t * wide, wide), wide)
        dots, squares = dots_of(mine, where)
        mass[:, where] = dots
        norms[:, where] = squares
        return carry

    def more_dots(g):
        def body(t, carry):
            where = pl.ds(pl.multiple_of(t * wide, wide), wide)
            dots, squares = dots_of(g, where)
            mass[:, where] += dots
            norms[:, where] += squares
            return carry
        return body

    tiles = n_k // wide
    for e in (0, 1, -1, 3, -3, 2, -2):
        gx_got(e, 2).wait_recv()
    lax.fori_loop(0, tiles, first_dots, 0)
    for e in (6, -6, 4, -4, 5, -5, 7, -7):
        gx_got(e, 2).wait_recv()
    lax.fori_loop(0, tiles, more_dots((mine + 1) % 4), 0)
    lax.fori_loop(0, tiles, more_dots((mine + 3) % 4), 0)
    gx_got(8, 2).wait_recv()
    top[...] = jnp.full(top.shape, -jnp.inf, F32)

    def logits(t, carry):
        where = pl.ds(pl.multiple_of(t * wide, wide), wide)
        dots, squares = dots_of((mine + 2) % 4, where)
        score = (2.0 * (mass[:, where] + dots) - (norms[:, where] + squares)) * 1.25
        mass[:, where] = score
        best = score[:, :L]
        for i in range(1, wide // L):
            best = jnp.maximum(best, score[:, i * L:(i + 1) * L])
        top[...] = jnp.maximum(top[...], best)
        return carry

    lax.fori_loop(0, tiles, logits, 0)

    for e, root in sent_z:
        gz(e, root).wait_send()
    for e, frm, side in sent_x:
        gx(e, frm, side).wait_send()

    def swap(buf, slot, n, me, peer, send, recv):
        def copy(o):
            return pltpu.make_async_remote_copy(
                src_ref=buf.at[me], dst_ref=buf.at[me], send_sem=send.at[slot, o],
                recv_sem=recv.at[slot, o], device_id=peer(o), device_id_type=MESH)

        def start(o, carry):
            copy(o).start()
            return carry

        def wait(o, carry):
            copy(o).wait()
            return carry

        return (lambda: lax.fori_loop(1, n, start, 0)), (lambda: lax.fori_loop(1, n, wait, 0))

    def total(buf, n):
        out = buf[0]
        for i in range(1, n):
            out = out + buf[i]
        return out

    def row_block(j):
        return pl.ds(pl.multiple_of(j * L, L), L)

    def weigh(j, carry):
        block = top[row_block(j), :]
        peak = jnp.max(block, axis=1, keepdims=True)
        soft[c, pl.ds(j, 1), :] = jnp.max(block.T, axis=0, keepdims=True)
        acc = jnp.zeros((L, L), F32)
        for t in range(col_tiles):
            w = jnp.exp(mass[row_block(j), t * L:(t + 1) * L] - peak)
            mass[row_block(j), t * L:(t + 1) * L] = w
            acc = acc + w
        soft[c, pl.ds(row_blocks + j, 1), :] = jnp.sum(acc.T, axis=0, keepdims=True)
        return carry

    lax.fori_loop(0, row_blocks, weigh, 0)
    start, wait = swap(soft, 0, nc, c, cen_peer, soft_send, soft_recv)
    start()
    wait()
    peaks = soft[0, :row_blocks]
    for i in range(1, nc):
        peaks = jnp.maximum(peaks, soft[i, :row_blocks])
    sums = jnp.zeros_like(peaks)
    for i in range(nc):
        sums = sums + soft[i, row_blocks:] * jnp.exp(soft[i, :row_blocks] - peaks)
    scale_rows = jnp.exp(soft[c, :row_blocks] - peaks) / sums

    def spread(scales, j):
        return jnp.broadcast_to(scales[j:j + 1, :], (L, L)).T

    def add_down(v):
        return jnp.sum(v, axis=0, keepdims=True)

    def reduce_cols(slot):
        start_a, wait_a = swap(cols_a.at[slot], slot, na, ga, a_peer, ca_send, ca_recv)
        start_b, wait_b = swap(cols_b.at[slot], slot, zb, gb, b_peer, cb_send, cb_recv)

        def middle():
            wait_a()
            cols_b[slot, gb] = total(cols_a.at[slot], na)
            start_b()

        def last():
            wait_b()
            return total(cols_b.at[slot], zb)

        return start_a, middle, last

    for turn_no in range(PASSES):
        acc = [jnp.zeros((1, L), F32) for _ in range(col_tiles)]
        for j in range(row_blocks):
            scale = spread(scale_rows, j)
            for t in range(col_tiles):
                m = mass[j * L:(j + 1) * L, t * L:(t + 1) * L] * scale
                mass[j * L:(j + 1) * L, t * L:(t + 1) * L] = m
                acc[t] = acc[t] + add_down(m)
        for t in range(col_tiles):
            cols_a[turn_no, ga, t:t + 1, :] = acc[t]
        first, middle, last = reduce_cols(turn_no)
        first()
        middle()
        scale_cols = 1.0 / last()
        for j in range(row_blocks):
            acc_r = jnp.zeros((L, L), F32)
            for t in range(col_tiles):
                m = mass[j * L:(j + 1) * L, t * L:(t + 1) * L] * scale_cols[t:t + 1, :]
                mass[j * L:(j + 1) * L, t * L:(t + 1) * L] = m
                acc_r = acc_r + m
            rows[turn_no, c, j:j + 1, :] = add_down(acc_r.T)
        start, wait = swap(rows.at[turn_no], turn_no, nc, c, cen_peer, row_send, row_recv)
        start()
        wait()
        scale_rows = 1.0 / total(rows.at[turn_no], nc)

    acc = [jnp.zeros((1, L), F32) for _ in range(col_tiles)]
    for j in range(row_blocks):
        scale = spread(scale_rows, j)
        for t in range(col_tiles):
            m = (mass[j * L:(j + 1) * L, t * L:(t + 1) * L] * scale).astype(BF16)
            assign[j * L:(j + 1) * L, t * L:(t + 1) * L] = m
            acc[t] = acc[t] + add_down(m.astype(F32))
    store = pltpu.make_async_copy(assign, assign_ref, local_sem.at[1])
    store.start()
    for t in range(col_tiles):
        cols_a[PASSES, ga, t:t + 1, :] = acc[t]
    first, middle, last = reduce_cols(PASSES)
    first()

    def rx(first, n, o):
        k = first + 7
        return pltpu.make_async_remote_copy(
            src_ref=xsend.at[pl.ds(k, n), (x + o) % nx], dst_ref=xrecv.at[o - 1, pl.ds(k, n)],
            send_sem=rx_send.at[o - 1, k], recv_sem=rx_recv.at[o - 1, k],
            device_id=x_peer(o), device_id_type=MESH)

    def rz(e):
        return pltpu.make_async_remote_copy(
            src_ref=own.at[e + 7], dst_ref=zrecv.at[e + 7], send_sem=rz_send.at[e + 7], recv_sem=rz_recv.at[e + 7],
            device_id=z_peer(VIA.get(e, e)), device_id_type=MESH)

    peers = sorted(range(1, nx), key=lambda o: -min(o, nx - o))
    block = nx * chunk
    for first, n in PARTS:
        depth_rows = pl.ds(pl.multiple_of(((z + nz + first) % nz) * block, block), n * block)
        k = first + 7

        def product(t, carry):
            where = pl.ds(pl.multiple_of(t * wide, wide), wide)
            part = jnp.dot(pts_t[depth_rows, :], assign[:, where], preferred_element_type=F32)
            part = part.reshape(n, nx, chunk, wide)
            prod[k:k + n, :, :, where] = part
            xsend[k:k + n, :, :, where] = part.astype(BF16)
            return carry

        lax.fori_loop(0, tiles, product, 0)
        for o in peers:
            rx(first, n, o).start()

    def centre(e):
        v = own[e + 7]
        for f in FEEDS[e]:
            rz(f).wait_recv()
            v = v + zrecv[f + 7]
        own[e + 7] = v
        rz(e).start()

    for i, (first, n) in enumerate(PARTS):
        for o in peers:
            rx(first, n, o).wait_recv()
        for e in range(first, first + n):
            v = prod[e + 7, x]
            for o in range(1, nx):
                v = v + xrecv[o - 1, e + 7].astype(F32)
            own[e + 7] = v
            if e in VIA:
                rz(e).start()
        if i:
            before = PARTS[i - 1]
            for e in FEEDS:
                if before[0] <= e < before[0] + before[1]:
                    centre(e)
        else:
            middle()
    counts = last()
    numer = own[7]
    for e in (1, -1) + FAR:
        rz(e).wait_recv()
        numer = numer + zrecv[e + 7]
    for t in range(col_tiles):
        newc_ref[:, t * L:(t + 1) * L] = numer[:, t * L:(t + 1) * L] / counts[t:t + 1, :]
    for e in range(-7, 9):
        if e:
            rz(e).wait_send()
    for first, n in PARTS:
        for o in peers:
            rx(first, n, o).wait_send()
    store.wait()


def on_device(nx, nz, nc, za, points, centroids_t):
    n_rows, n_d = points.shape
    chunk, n_k = centroids_t.shape
    na, zb = za * nx, nz // za
    rb, ct = n_rows // L, n_k // L
    assert nz == 16
    vmem = pltpu.VMEM
    dma = pltpu.SemaphoreType.DMA
    return pl.pallas_call(
        functools.partial(kernel, nx, nz, nc, za),
        out_shape=(
            jax.ShapeDtypeStruct((chunk, n_k), F32),
            jax.ShapeDtypeStruct((n_rows, n_k), BF16),
        ),
        in_specs=[pl.BlockSpec(memory_space=pl.ANY), pl.BlockSpec(memory_space=vmem)],
        out_specs=(pl.BlockSpec(memory_space=vmem), pl.BlockSpec(memory_space=pl.ANY)),
        scratch_shapes=[
            vmem((n_rows, n_d), BF16),
            vmem((n_d + 3 * nx * chunk, n_rows), BF16),
            vmem((n_d, n_k), BF16),
            vmem((n_rows, n_k), F32),
            vmem((1, n_k), F32),
            vmem((n_rows, L), F32),
            vmem((n_rows, n_k), BF16),
            vmem((nz, chunk, n_k), F32),
            vmem((nz, nx, chunk, n_k), F32),
            vmem((nz, nx, chunk, n_k), BF16),
            vmem((nx - 1, nz, chunk, n_k), BF16),
            vmem((nz, chunk, n_k), F32),
            vmem((nc, 2 * rb, L), F32),
            vmem((PASSES, nc, rb, L), F32),
            vmem((PASSES + 1, na, ct, L), F32),
            vmem((PASSES + 1, zb, ct, L), F32),
            dma((2,)),
            dma((nz, 3)), dma((nz, 3)),
            dma((nz,)), dma((nz,)),
            dma((1, nc)), dma((1, nc)),
            dma((PASSES, nc)), dma((PASSES, nc)),
            dma((PASSES + 1, na)), dma((PASSES + 1, na)),
            dma((PASSES + 1, zb)), dma((PASSES + 1, zb)),
            dma((nx - 1, nz)), dma((nx - 1, nz)),
            dma((nz,)), dma((nz,)),
        ],
        compiler_params=pltpu.CompilerParams(
            collective_id=0, has_side_effects=True, vmem_limit_bytes=50 * 1024 * 1024
        ),
    )(points, centroids_t)


def solution(mesh, nx=X_CHIPS, za=Z_GROUP):
    nz = mesh.shape["pts"] // nx
    return jax.shard_map(
        functools.partial(on_device, nx, nz, mesh.shape["cen"], za),
        mesh=mesh,
        in_specs=(P("pts", None), P("pts", "cen")),
        out_specs=(P("pts", "cen"), P("pts", "cen")),
        check_vma=False,
    )
```

```python
import functools

import jax
import jax.numpy as jnp
from jax import lax
from jax.experimental import pallas as pl
from jax.experimental.pallas import tpu as pltpu
from jax.sharding import PartitionSpec as P

PASSES = 3
MESH = pl.DeviceIdType.MESH
L = 128
F32 = jnp.float32
BF16 = jnp.bfloat16
X_CHIPS = 4
Z_GROUP = 2
VIA = {1: 1, -1: -1, 2: -1, 4: 1, 5: -1, 7: 1, 8: 2, -2: 1, -4: -1, -5: 1, -7: -1}
FEEDS = {6: (7, 5, 8), -6: (-7, -5), 3: (4, 2, 6), -3: (-4, -2, -6)}
STEP = {6: 3, -6: -3, 3: 3, -3: -3}
FAR = (6, -6, 3, -3)
GREET_Z = (1, -1, 2, -2, 3, -3, 6, -6)
PARTS = ((5, 4), (-7, 3), (2, 3), (-4, 3), (-1, 3))


def kernel(nx, nz, nc, za, points_ref, cent_ref, newc_ref, assign_ref,
           pts, pts_t, piece, mass, norms, top, assign, own, prod, xfar, xfar_in, xsend, xrecv, zrecv,
           soft, rows, cols_a, cols_b,
           local_sem, gx_send, gx_recv, gz_send, gz_recv, soft_send, soft_recv,
           row_send, row_recv, ca_send, ca_recv, cb_send, cb_recv,
           rx1_send, rx1_recv, rx2_send, rx2_recv, rz_send, rz_recv):
    n_rows, n_d = points_ref.shape
    chunk, n_k = cent_ref.shape
    row_blocks = n_rows // L
    col_tiles = n_k // L
    wide = min(256, n_k)
    zb = nz // za
    na = za * nx

    p = lax.axis_index("pts")
    c = lax.axis_index("cen")
    z = p // nx
    x = p % nx
    ga = (z % za) * nx + x
    gb = z // za

    def cen_peer(o):
        return {"cen": (c + o) % nc}

    def a_peer(o):
        q = (ga + o) % na
        return {"pts": ((z // za) * za + q // nx) * nx + q % nx}

    def b_peer(o):
        return {"pts": (((gb + o) % zb) * za + z % za) * nx + x}

    def x_peer(o):
        return {"pts": z * nx + (x + o) % nx}

    def z_peer(o):
        return {"pts": ((z + nz + o) % nz) * nx + x}

    load = pltpu.make_async_copy(points_ref, pts, local_sem.at[0])
    load.start()

    barrier = pltpu.get_barrier_semaphore()

    def greet(peer, n):
        def body(o, carry):
            pl.semaphore_signal(barrier, inc=1, device_id=peer(o), device_id_type=MESH)
            return carry
        lax.fori_loop(1, n, body, 0)

    greet(cen_peer, nc)
    greet(x_peer, nx)
    for e in GREET_Z:
        pl.semaphore_signal(barrier, inc=1, device_id=z_peer(e), device_id_type=MESH)
    pl.semaphore_wait(barrier, (nc - 1) + (nx - 1) + len(GREET_Z))

    def slab(e, side):
        first = ((z + nz + e) % nz) * nx + (x + nx + side) % nx
        return piece.at[pl.ds(pl.multiple_of(first * chunk, chunk), chunk), :]

    piece[pl.ds(pl.multiple_of(p * chunk, chunk), chunk), :] = cent_ref[...]

    def gz(e, root):
        at = root - e + 7
        at = at + nz if at < 0 else at - nz if at >= nz else at
        part = slab(root, 0)
        return pltpu.make_async_remote_copy(
            src_ref=part, dst_ref=part, send_sem=gz_send.at[at], recv_sem=gz_recv.at[at],
            device_id=z_peer(e), device_id_type=MESH)

    def gz_got(e):
        part = slab(e, 0)
        return pltpu.make_async_remote_copy(
            src_ref=part, dst_ref=part, send_sem=gz_send.at[e + 7], recv_sem=gz_recv.at[e + 7],
            device_id=z_peer(1), device_id_type=MESH)

    def gx(e, frm, side):
        part = slab(e, frm)
        lane = 0 if frm == 0 and side == 1 else 1 if frm == 0 else 2
        return pltpu.make_async_remote_copy(
            src_ref=part, dst_ref=part, send_sem=gx_send.at[e + 7, lane], recv_sem=gx_recv.at[e + 7, lane],
            device_id=x_peer(nx + side), device_id_type=MESH)

    def gx_got(e, lane):
        part = slab(e, (-1, 1, 2)[lane])
        return pltpu.make_async_remote_copy(
            src_ref=part, dst_ref=part, send_sem=gx_send.at[e + 7, lane], recv_sem=gx_recv.at[e + 7, lane],
            device_id=x_peer(1), device_id_type=MESH)

    sent_z = []
    sent_x = []

    def go_z(e, root):
        gz(e, root).start()
        sent_z.append((e, root))

    def go_x(e, frm, side):
        gx(e, frm, side).start()
        sent_x.append((e, frm, side))

    def x_near(e):
        go_x(e, 0, 1)
        go_x(e, 0, -1)

    def x_on(e):
        gx_got(e, 0).wait_recv()
        gx_got(e, 1).wait_recv()
        if e % 2 == 0:
            go_x(e, -1, 1)
        else:
            go_x(e, 1, -1)

    d_blocks = n_d // L

    def turn(b):
        block = pts[:, pl.ds(pl.multiple_of(b * L, L), L)].astype(F32)
        pts_t[pl.ds(pl.multiple_of(b * L, L), L), :] = block.T.astype(BF16)

    def turns(first, last):
        def body(b, carry):
            turn(b)
            return carry
        lax.fori_loop(first, last, body, 0)

    for e in FAR + (1, -1):
        go_z(e, 0)
    x_near(0)
    load.wait()
    turns(0, d_blocks // 2)
    for e in (1, -1):
        gz_got(e).wait_recv()
        x_near(e)
    for e in (3, -3):
        gz_got(e).wait_recv()
        go_z(1, e)
        go_z(-1, e)
        x_near(e)
    x_on(0)
    for e in (6, -6):
        gz_got(e).wait_recv()
        go_z(1, e)
        go_z(-1, e)
        if e == -6:
            go_z(2, e)
        x_near(e)
    for e in (1, -1, 3, -3):
        x_on(e)
    for e in (2, -2, 4, -4):
        gz_got(e).wait_recv()
        x_near(e)
    x_on(6)
    x_on(-6)
    for e in (5, -5, 7, -7, 8):
        gz_got(e).wait_recv()
        x_near(e)
    turns(d_blocks // 2, d_blocks)
    ahead = 3 * nx * chunk
    pts_t[n_d:n_d + ahead, :] = pts_t[:ahead, :]
    for e in (2, -2, 4, -4):
        x_on(e)

    quarter = n_d // 4
    mine = z // (nz // 4)

    def depth(g):
        return pl.ds(pl.multiple_of(g * quarter, quarter), quarter)

    def dots_of(g, where):
        part = piece[depth(g), where]
        long = part.astype(F32)
        dots = jnp.dot(pts[:, depth(g)], part, preferred_element_type=F32)
        return dots, jnp.sum(long * long, axis=0, keepdims=True)

    def first_dots(t, carry):
        where = pl.ds(pl.multiple_of(t * wide, wide), wide)
        dots, squares = dots_of(mine, where)
        mass[:, where] = dots
        norms[:, where] = squares
        return carry

    def more_dots(g):
        def body(t, carry):
            where = pl.ds(pl.multiple_of(t * wide, wide), wide)
            dots, squares = dots_of(g, where)
            mass[:, where] += dots
            norms[:, where] += squares
            return carry
        return body

    tiles = n_k // wide
    for e in (0, 1, -1, 3, -3, 2, -2):
        gx_got(e, 2).wait_recv()
    lax.fori_loop(0, tiles, first_dots, 0)
    for e in (5, -5, 7, -7, 8):
        x_on(e)
    for e in (6, -6, 4, -4, 5, -5, 7, -7):
        gx_got(e, 2).wait_recv()
    lax.fori_loop(0, tiles, more_dots((mine + 1) % 4), 0)
    lax.fori_loop(0, tiles, more_dots((mine + 3) % 4), 0)
    gx_got(8, 2).wait_recv()
    top[...] = jnp.full(top.shape, -jnp.inf, F32)

    def logits(t, carry):
        where = pl.ds(pl.multiple_of(t * wide, wide), wide)
        dots, squares = dots_of((mine + 2) % 4, where)
        score = (2.0 * (mass[:, where] + dots) - (norms[:, where] + squares)) * 1.25
        mass[:, where] = score
        best = score[:, :L]
        for i in range(1, wide // L):
            best = jnp.maximum(best, score[:, i * L:(i + 1) * L])
        top[...] = jnp.maximum(top[...], best)
        return carry

    lax.fori_loop(0, tiles, logits, 0)

    for e, root in sent_z:
        gz(e, root).wait_send()
    for e, frm, side in sent_x:
        gx(e, frm, side).wait_send()

    def swap(buf, slot, n, me, peer, send, recv):
        def copy(o):
            return pltpu.make_async_remote_copy(
                src_ref=buf.at[me], dst_ref=buf.at[me], send_sem=send.at[slot, o],
                recv_sem=recv.at[slot, o], device_id=peer(o), device_id_type=MESH)

        def start(o, carry):
            copy(o).start()
            return carry

        def wait(o, carry):
            copy(o).wait()
            return carry

        return (lambda: lax.fori_loop(1, n, start, 0)), (lambda: lax.fori_loop(1, n, wait, 0))

    def total(buf, n):
        out = buf[0]
        for i in range(1, n):
            out = out + buf[i]
        return out

    def row_block(j):
        return pl.ds(pl.multiple_of(j * L, L), L)

    def weigh(j, carry):
        block = top[row_block(j), :]
        peak = jnp.max(block, axis=1, keepdims=True)
        soft[c, pl.ds(j, 1), :] = jnp.max(block.T, axis=0, keepdims=True)
        acc = jnp.zeros((L, L), F32)
        for t in range(col_tiles):
            w = jnp.exp(mass[row_block(j), t * L:(t + 1) * L] - peak)
            mass[row_block(j), t * L:(t + 1) * L] = w
            acc = acc + w
        soft[c, pl.ds(row_blocks + j, 1), :] = jnp.sum(acc.T, axis=0, keepdims=True)
        return carry

    lax.fori_loop(0, row_blocks, weigh, 0)
    start, wait = swap(soft, 0, nc, c, cen_peer, soft_send, soft_recv)
    start()
    wait()
    peaks = soft[0, :row_blocks]
    for i in range(1, nc):
        peaks = jnp.maximum(peaks, soft[i, :row_blocks])
    sums = jnp.zeros_like(peaks)
    for i in range(nc):
        sums = sums + soft[i, row_blocks:] * jnp.exp(soft[i, :row_blocks] - peaks)
    scale_rows = jnp.exp(soft[c, :row_blocks] - peaks) / sums

    def spread(scales, j):
        return jnp.broadcast_to(scales[j:j + 1, :], (L, L)).T

    def add_down(v):
        return jnp.sum(v, axis=0, keepdims=True)

    def reduce_cols(slot):
        start_a, wait_a = swap(cols_a.at[slot], slot, na, ga, a_peer, ca_send, ca_recv)
        start_b, wait_b = swap(cols_b.at[slot], slot, zb, gb, b_peer, cb_send, cb_recv)

        def middle():
            wait_a()
            cols_b[slot, gb] = total(cols_a.at[slot], na)
            start_b()

        def last():
            wait_b()
            return total(cols_b.at[slot], zb)

        return start_a, middle, last

    for turn_no in range(PASSES):
        acc = [jnp.zeros((1, L), F32) for _ in range(col_tiles)]
        for j in range(row_blocks):
            scale = spread(scale_rows, j)
            for t in range(col_tiles):
                m = mass[j * L:(j + 1) * L, t * L:(t + 1) * L] * scale
                mass[j * L:(j + 1) * L, t * L:(t + 1) * L] = m
                acc[t] = acc[t] + add_down(m)
        for t in range(col_tiles):
            cols_a[turn_no, ga, t:t + 1, :] = acc[t]
        first, middle, last = reduce_cols(turn_no)
        first()
        middle()
        scale_cols = 1.0 / last()
        for j in range(row_blocks):
            acc_r = jnp.zeros((L, L), F32)
            for t in range(col_tiles):
                m = mass[j * L:(j + 1) * L, t * L:(t + 1) * L] * scale_cols[t:t + 1, :]
                mass[j * L:(j + 1) * L, t * L:(t + 1) * L] = m
                acc_r = acc_r + m
            rows[turn_no, c, j:j + 1, :] = add_down(acc_r.T)
        start, wait = swap(rows.at[turn_no], turn_no, nc, c, cen_peer, row_send, row_recv)
        start()
        wait()
        scale_rows = 1.0 / total(rows.at[turn_no], nc)

    acc = [jnp.zeros((1, L), F32) for _ in range(col_tiles)]
    for j in range(row_blocks):
        scale = spread(scale_rows, j)
        for t in range(col_tiles):
            m = (mass[j * L:(j + 1) * L, t * L:(t + 1) * L] * scale).astype(BF16)
            assign[j * L:(j + 1) * L, t * L:(t + 1) * L] = m
            acc[t] = acc[t] + add_down(m.astype(F32))
    store = pltpu.make_async_copy(assign, assign_ref, local_sem.at[1])
    store.start()
    for t in range(col_tiles):
        cols_a[PASSES, ga, t:t + 1, :] = acc[t]
    first, middle, last = reduce_cols(PASSES)
    first()

    half = n_k // 2

    def rx1(first, n, side):
        k = first + 7
        return pltpu.make_async_remote_copy(
            src_ref=xfar.at[side, pl.ds(k, n)], dst_ref=xfar_in.at[side, pl.ds(k, n)],
            send_sem=rx1_send.at[side, k], recv_sem=rx1_recv.at[side, k],
            device_id=x_peer(1 if side == 0 else nx - 1), device_id_type=MESH)

    def rx2(first, n, side):
        k = first + 7
        return pltpu.make_async_remote_copy(
            src_ref=xsend.at[side, pl.ds(k, n)], dst_ref=xrecv.at[side, pl.ds(k, n)],
            send_sem=rx2_send.at[side, k], recv_sem=rx2_recv.at[side, k],
            device_id=x_peer(1 if side == 0 else nx - 1), device_id_type=MESH)

    def rz(e):
        return pltpu.make_async_remote_copy(
            src_ref=own.at[e + 7], dst_ref=zrecv.at[e + 7], send_sem=rz_send.at[e + 7], recv_sem=rz_recv.at[e + 7],
            device_id=z_peer(VIA[e] if e in VIA else STEP[e]), device_id_type=MESH)

    block = nx * chunk
    for first, n in PARTS:
        depth_rows = pl.ds(pl.multiple_of(((z + nz + first) % nz) * block, block), n * block)
        k = first + 7

        def product(t, carry):
            where = pl.ds(pl.multiple_of(t * wide, wide), wide)
            part = jnp.dot(pts_t[depth_rows, :], assign[:, where], preferred_element_type=F32)
            prod[k:k + n, :, :, where] = part.reshape(n, nx, chunk, wide)
            return carry

        lax.fori_loop(0, tiles, product, 0)
        for e in range(first, first + n):
            far = prod[e + 7, (x + 2) % nx].astype(BF16)
            xfar[0, e + 7] = far[:, :half]
            xfar[1, e + 7] = far[:, half:]
        for side in range(2):
            rx1(first, n, side).start()

    def forward(first, n):
        for side in range(2):
            rx1(first, n, side).wait_recv()
        for side in range(2):
            for e in range(first, first + n):
                v = prod[e + 7, (x + 1 + 2 * side) % nx]
                w = xfar_in[side, e + 7].astype(F32)
                if side == 0:
                    xsend[side, e + 7, :, :half] = (v[:, :half] + w).astype(BF16)
                    xsend[side, e + 7, :, half:] = v[:, half:].astype(BF16)
                else:
                    xsend[side, e + 7, :, :half] = v[:, :half].astype(BF16)
                    xsend[side, e + 7, :, half:] = (v[:, half:] + w).astype(BF16)
            rx2(first, n, side).start()

    def centre(e):
        v = own[e + 7]
        for f in FEEDS[e]:
            rz(f).wait_recv()
            v = v + zrecv[f + 7]
        own[e + 7] = v
        rz(e).start()

    forward(*PARTS[0])
    forward(*PARTS[1])
    for i, (first, n) in enumerate(PARTS):
        for side in range(2):
            rx2(first, n, side).wait_recv()
        for e in range(first, first + n):
            own[e + 7] = prod[e + 7, x] + xrecv[0, e + 7].astype(F32) + xrecv[1, e + 7].astype(F32)
            if e in VIA:
                rz(e).start()
        if i + 2 < len(PARTS):
            forward(*PARTS[i + 2])
        if i:
            before = PARTS[i - 1]
            for e in FEEDS:
                if before[0] <= e < before[0] + before[1]:
                    centre(e)
        else:
            middle()
    counts = last()
    numer = own[7]
    for e in (1, -1, 3, -3):
        rz(e).wait_recv()
        numer = numer + zrecv[e + 7]
    for t in range(col_tiles):
        newc_ref[:, t * L:(t + 1) * L] = numer[:, t * L:(t + 1) * L] / counts[t:t + 1, :]
    for e in range(-7, 9):
        if e:
            rz(e).wait_send()
    for first, n in PARTS:
        for side in range(2):
            rx1(first, n, side).wait_send()
            rx2(first, n, side).wait_send()
    store.wait()


def on_device(nx, nz, nc, za, points, centroids_t):
    n_rows, n_d = points.shape
    chunk, n_k = centroids_t.shape
    na, zb = za * nx, nz // za
    rb, ct = n_rows // L, n_k // L
    assert nz == 16 and nx == 4
    vmem = pltpu.VMEM
    dma = pltpu.SemaphoreType.DMA
    return pl.pallas_call(
        functools.partial(kernel, nx, nz, nc, za),
        out_shape=(
            jax.ShapeDtypeStruct((chunk, n_k), F32),
            jax.ShapeDtypeStruct((n_rows, n_k), BF16),
        ),
        in_specs=[pl.BlockSpec(memory_space=pl.ANY), pl.BlockSpec(memory_space=vmem)],
        out_specs=(pl.BlockSpec(memory_space=vmem), pl.BlockSpec(memory_space=pl.ANY)),
        scratch_shapes=[
            vmem((n_rows, n_d), BF16),
            vmem((n_d + 3 * nx * chunk, n_rows), BF16),
            vmem((n_d, n_k), BF16),
            vmem((n_rows, n_k), F32),
            vmem((1, n_k), F32),
            vmem((n_rows, L), F32),
            vmem((n_rows, n_k), BF16),
            vmem((nz, chunk, n_k), F32),
            vmem((nz, nx, chunk, n_k), F32),
            vmem((2, nz, chunk, n_k // 2), BF16),
            vmem((2, nz, chunk, n_k // 2), BF16),
            vmem((2, nz, chunk, n_k), BF16),
            vmem((2, nz, chunk, n_k), BF16),
            vmem((nz, chunk, n_k), F32),
            vmem((nc, 2 * rb, L), F32),
            vmem((PASSES, nc, rb, L), F32),
            vmem((PASSES + 1, na, ct, L), F32),
            vmem((PASSES + 1, zb, ct, L), F32),
            dma((2,)),
            dma((nz, 3)), dma((nz, 3)),
            dma((nz,)), dma((nz,)),
            dma((1, nc)), dma((1, nc)),
            dma((PASSES, nc)), dma((PASSES, nc)),
            dma((PASSES + 1, na)), dma((PASSES + 1, na)),
            dma((PASSES + 1, zb)), dma((PASSES + 1, zb)),
            dma((2, nz)), dma((2, nz)),
            dma((2, nz)), dma((2, nz)),
            dma((nz,)), dma((nz,)),
        ],
        compiler_params=pltpu.CompilerParams(
            collective_id=0, has_side_effects=True, vmem_limit_bytes=50 * 1024 * 1024
        ),
    )(points, centroids_t)


def solution(mesh, nx=X_CHIPS, za=Z_GROUP):
    nz = mesh.shape["pts"] // nx
    return jax.shard_map(
        functools.partial(on_device, nx, nz, mesh.shape["cen"], za),
        mesh=mesh,
        in_specs=(P("pts", None), P("pts", "cen")),
        out_specs=(P("pts", "cen"), P("pts", "cen")),
        check_vma=False,
    )
```

```python
import functools

import jax
import jax.numpy as jnp
from jax import lax
from jax.experimental import pallas as pl
from jax.experimental.pallas import tpu as pltpu
from jax.sharding import PartitionSpec as P

PASSES = 3
MESH = pl.DeviceIdType.MESH
L = 128
F32 = jnp.float32
BF16 = jnp.bfloat16
X_CHIPS = 4
VIA = {1: 1, -1: -1, 2: -1, 4: 1, 5: -1, 7: 1, 8: 2, -2: 1, -4: -1, -5: 1, -7: -1}
FEEDS = {6: (7, 5, 8), -6: (-7, -5), 3: (4, 2, 6), -3: (-4, -2, -6)}
STEP = {6: 3, -6: -3, 3: 3, -3: -3}
GREET_Z = (1, -1, 2, -2, 3, -3)
CENTRES = (6, -6, 3, -3)
PARTS = ((5, 4), (-7, 3), (2, 3), (-4, 3), (-1, 3))


def kernel(nx, nz, nc, points_ref, cent_ref, newc_ref, assign_ref,
           pts, pts_t, piece, mass, norms, top, assign, own, prod, xfar, xfar_in, xsend, xrecv, zrecv,
           soft, rows, cols_a, cols_b,
           local_sem, gx_send, gx_recv, gz_send, gz_recv, soft_send, soft_recv,
           row_send, row_recv, ca_send, ca_recv, cb_send, cb_recv,
           rx1_send, rx1_recv, rx2_send, rx2_recv, rz_send, rz_recv):
    n_rows, n_d = points_ref.shape
    chunk, n_k = cent_ref.shape
    row_blocks = n_rows // L
    col_tiles = n_k // L
    wide = min(256, n_k)

    p = lax.axis_index("pts")
    c = lax.axis_index("cen")
    z = p // nx
    x = p % nx

    def cen_peer(o):
        return {"cen": (c + o) % nc}

    def x_peer(o):
        return {"pts": z * nx + (x + o) % nx}

    def z_peer(o):
        return {"pts": ((z + nz + o) % nz) * nx + x}

    load = pltpu.make_async_copy(points_ref, pts, local_sem.at[0])
    load.start()

    barrier = pltpu.get_barrier_semaphore()

    def greet(peer, n):
        def body(o, carry):
            pl.semaphore_signal(barrier, inc=1, device_id=peer(o), device_id_type=MESH)
            return carry
        lax.fori_loop(1, n, body, 0)

    greet(cen_peer, nc)
    greet(x_peer, nx)
    for e in GREET_Z:
        pl.semaphore_signal(barrier, inc=1, device_id=z_peer(e), device_id_type=MESH)
    pl.semaphore_wait(barrier, (nc - 1) + (nx - 1) + len(GREET_Z))

    def slab(e, side):
        first = ((z + nz + e) % nz) * nx + (x + nx + side) % nx
        return piece.at[pl.ds(pl.multiple_of(first * chunk, chunk), chunk), :]

    piece[pl.ds(pl.multiple_of(p * chunk, chunk), chunk), :] = cent_ref[...]

    def gz(e, root):
        at = root - e + 7
        at = at + nz if at < 0 else at - nz if at >= nz else at
        part = slab(root, 0)
        return pltpu.make_async_remote_copy(
            src_ref=part, dst_ref=part, send_sem=gz_send.at[at], recv_sem=gz_recv.at[at],
            device_id=z_peer(e), device_id_type=MESH)

    def gz_got(e):
        part = slab(e, 0)
        return pltpu.make_async_remote_copy(
            src_ref=part, dst_ref=part, send_sem=gz_send.at[e + 7], recv_sem=gz_recv.at[e + 7],
            device_id=z_peer(1), device_id_type=MESH)

    def gx(e, frm, side):
        part = slab(e, frm)
        lane = 0 if frm == 0 and side == 1 else 1 if frm == 0 else 2
        return pltpu.make_async_remote_copy(
            src_ref=part, dst_ref=part, send_sem=gx_send.at[e + 7, lane], recv_sem=gx_recv.at[e + 7, lane],
            device_id=x_peer(nx + side), device_id_type=MESH)

    def gx_got(e, lane):
        part = slab(e, (-1, 1, 2)[lane])
        return pltpu.make_async_remote_copy(
            src_ref=part, dst_ref=part, send_sem=gx_send.at[e + 7, lane], recv_sem=gx_recv.at[e + 7, lane],
            device_id=x_peer(1), device_id_type=MESH)

    sent_z = []
    sent_x = []

    def go_z(e, root):
        gz(e, root).start()
        sent_z.append((e, root))

    def go_x(e, frm, side):
        gx(e, frm, side).start()
        sent_x.append((e, frm, side))

    def x_near(e):
        go_x(e, 0, 1)
        go_x(e, 0, -1)

    def x_on(e):
        gx_got(e, 0).wait_recv()
        gx_got(e, 1).wait_recv()
        if e % 2 == 0:
            go_x(e, -1, 1)
        else:
            go_x(e, 1, -1)

    d_blocks = n_d // L

    def turn(b):
        block = pts[:, pl.ds(pl.multiple_of(b * L, L), L)].astype(F32)
        pts_t[pl.ds(pl.multiple_of(b * L, L), L), :] = block.T.astype(BF16)

    def turns(first, last):
        def body(b, carry):
            turn(b)
            return carry
        lax.fori_loop(first, last, body, 0)

    for e in (3, -3, 1, -1):
        go_z(e, 0)
    x_near(0)
    load.wait()
    turns(0, d_blocks // 2)
    for e in (1, -1):
        gz_got(e).wait_recv()
        x_near(e)
    for e in (3, -3):
        gz_got(e).wait_recv()
        go_z(-e, e)
        go_z(1, e)
        go_z(-1, e)
        x_near(e)
    x_on(0)
    x_on(1)
    x_on(-1)
    for e in (2, -2, 4, -4):
        gz_got(e).wait_recv()
        x_near(e)
    for e in (6, -6):
        gz_got(e).wait_recv()
        go_z(1, e)
        go_z(-1, e)
        if e == -6:
            go_z(2, e)
        x_near(e)
    for e in (3, -3, 2, -2, 4, -4):
        x_on(e)
    for e in (5, -5, 7, -7, 8):
        gz_got(e).wait_recv()
        x_near(e)
    turns(d_blocks // 2, d_blocks)
    ahead = 3 * nx * chunk
    pts_t[n_d:n_d + ahead, :] = pts_t[:ahead, :]
    x_on(6)
    x_on(-6)

    quarter = n_d // 4
    mine = z // (nz // 4)

    def depth(g):
        return pl.ds(pl.multiple_of(g * quarter, quarter), quarter)

    def dots_of(g, where):
        part = piece[depth(g), where]
        long = part.astype(F32)
        dots = jnp.dot(pts[:, depth(g)], part, preferred_element_type=F32)
        return dots, jnp.sum(long * long, axis=0, keepdims=True)

    def first_dots(t, carry):
        where = pl.ds(pl.multiple_of(t * wide, wide), wide)
        dots, squares = dots_of(mine, where)
        mass[:, where] = dots
        norms[:, where] = squares
        return carry

    def more_dots(g):
        def body(t, carry):
            where = pl.ds(pl.multiple_of(t * wide, wide), wide)
            dots, squares = dots_of(g, where)
            mass[:, where] += dots
            norms[:, where] += squares
            return carry
        return body

    tiles = n_k // wide
    for e in (0, 1, -1, 3, -3, 2, -2):
        gx_got(e, 2).wait_recv()
    lax.fori_loop(0, tiles, first_dots, 0)
    for e in (5, -5, 7, -7, 8):
        x_on(e)
    for e in (6, -6, 4, -4, 5, -5, 7, -7):
        gx_got(e, 2).wait_recv()
    lax.fori_loop(0, tiles, more_dots((mine + 1) % 4), 0)
    lax.fori_loop(0, tiles, more_dots((mine + 3) % 4), 0)
    gx_got(8, 2).wait_recv()
    top[...] = jnp.full(top.shape, -jnp.inf, F32)

    def logits(t, carry):
        where = pl.ds(pl.multiple_of(t * wide, wide), wide)
        dots, squares = dots_of((mine + 2) % 4, where)
        score = (2.0 * (mass[:, where] + dots) - (norms[:, where] + squares)) * 1.25
        mass[:, where] = score
        best = score[:, :L]
        for i in range(1, wide // L):
            best = jnp.maximum(best, score[:, i * L:(i + 1) * L])
        top[...] = jnp.maximum(top[...], best)
        return carry

    lax.fori_loop(0, tiles, logits, 0)

    for e, root in sent_z:
        gz(e, root).wait_send()
    for e, frm, side in sent_x:
        gx(e, frm, side).wait_send()

    def swap(buf, slot, n, me, peer, send, recv):
        def copy(o):
            return pltpu.make_async_remote_copy(
                src_ref=buf.at[me], dst_ref=buf.at[me], send_sem=send.at[slot, o],
                recv_sem=recv.at[slot, o], device_id=peer(o), device_id_type=MESH)

        def start(o, carry):
            copy(o).start()
            return carry

        def wait(o, carry):
            copy(o).wait()
            return carry

        return (lambda: lax.fori_loop(1, n, start, 0)), (lambda: lax.fori_loop(1, n, wait, 0))

    def total(buf, n):
        out = buf[0]
        for i in range(1, n):
            out = out + buf[i]
        return out

    def row_block(j):
        return pl.ds(pl.multiple_of(j * L, L), L)

    def weigh(j, carry):
        block = top[row_block(j), :]
        peak = jnp.max(block, axis=1, keepdims=True)
        soft[c, pl.ds(j, 1), :] = jnp.max(block.T, axis=0, keepdims=True)
        acc = jnp.zeros((L, L), F32)
        for t in range(col_tiles):
            w = jnp.exp(mass[row_block(j), t * L:(t + 1) * L] - peak)
            mass[row_block(j), t * L:(t + 1) * L] = w
            acc = acc + w
        soft[c, pl.ds(row_blocks + j, 1), :] = jnp.sum(acc.T, axis=0, keepdims=True)
        return carry

    lax.fori_loop(0, row_blocks, weigh, 0)
    start, wait = swap(soft, 0, nc, c, cen_peer, soft_send, soft_recv)
    start()
    wait()
    peaks = soft[0, :row_blocks]
    for i in range(1, nc):
        peaks = jnp.maximum(peaks, soft[i, :row_blocks])
    sums = jnp.zeros_like(peaks)
    for i in range(nc):
        sums = sums + soft[i, row_blocks:] * jnp.exp(soft[i, :row_blocks] - peaks)
    scale_rows = jnp.exp(soft[c, :row_blocks] - peaks) / sums

    def spread(scales, j):
        return jnp.broadcast_to(scales[j:j + 1, :], (L, L)).T

    def add_down(v):
        return jnp.sum(v, axis=0, keepdims=True)

    near = [(d, o) for d in (1, -1, 0) for o in range(nx) if d or o]
    opposite = [(8, o) for o in range(nx)]

    def col_copy(slot, d, o):
        lane = (1 - d) * nx + o if d != 8 else 3 * nx + o
        there = (1 - d) * nx + x if d != 8 else 3 * nx + x
        return pltpu.make_async_remote_copy(
            src_ref=cols_a.at[slot, nx + x], dst_ref=cols_a.at[slot, there],
            send_sem=ca_send.at[slot, lane], recv_sem=ca_recv.at[slot, lane],
            device_id={"pts": ((z + nz + d) % nz) * nx + (x + o) % nx}, device_id_type=MESH)

    def centre_copy(slot, i, e):
        return pltpu.make_async_remote_copy(
            src_ref=cols_b.at[slot, 0], dst_ref=cols_b.at[slot, 1 + i],
            send_sem=cb_send.at[slot, i], recv_sem=cb_recv.at[slot, i],
            device_id=z_peer(e), device_id_type=MESH)

    def reduce_cols(slot):
        def first():
            for d, o in opposite + near:
                col_copy(slot, d, o).start()

        def middle():
            for d, o in near:
                col_copy(slot, d, o).wait_recv()
            cols_b[slot, 0] = total(cols_a.at[slot], 3 * nx)
            for i, e in enumerate(CENTRES):
                centre_copy(slot, i, e).start()

        def last():
            for d, o in opposite:
                col_copy(slot, d, o).wait_recv()
            out = cols_a[slot, 3 * nx]
            for i in range(1, nx):
                out = out + cols_a[slot, 3 * nx + i]
            for i, e in enumerate(CENTRES):
                centre_copy(slot, i, e).wait_recv()
            for i in range(len(CENTRES) + 1):
                out = out + cols_b[slot, i]
            for i, e in enumerate(CENTRES):
                centre_copy(slot, i, e).wait_send()
            for d, o in opposite + near:
                col_copy(slot, d, o).wait_send()
            return out

        return first, middle, last

    for turn_no in range(PASSES):
        acc = [jnp.zeros((1, L), F32) for _ in range(col_tiles)]
        for j in range(row_blocks):
            scale = spread(scale_rows, j)
            for t in range(col_tiles):
                m = mass[j * L:(j + 1) * L, t * L:(t + 1) * L] * scale
                mass[j * L:(j + 1) * L, t * L:(t + 1) * L] = m
                acc[t] = acc[t] + add_down(m)
        for t in range(col_tiles):
            cols_a[turn_no, nx + x, t:t + 1, :] = acc[t]
        first, middle, last = reduce_cols(turn_no)
        first()
        middle()
        scale_cols = 1.0 / last()
        for j in range(row_blocks):
            acc_r = jnp.zeros((L, L), F32)
            for t in range(col_tiles):
                m = mass[j * L:(j + 1) * L, t * L:(t + 1) * L] * scale_cols[t:t + 1, :]
                mass[j * L:(j + 1) * L, t * L:(t + 1) * L] = m
                acc_r = acc_r + m
            rows[turn_no, c, j:j + 1, :] = add_down(acc_r.T)
        start, wait = swap(rows.at[turn_no], turn_no, nc, c, cen_peer, row_send, row_recv)
        start()
        wait()
        scale_rows = 1.0 / total(rows.at[turn_no], nc)

    acc = [jnp.zeros((1, L), F32) for _ in range(col_tiles)]
    for j in range(row_blocks):
        scale = spread(scale_rows, j)
        for t in range(col_tiles):
            m = (mass[j * L:(j + 1) * L, t * L:(t + 1) * L] * scale).astype(BF16)
            assign[j * L:(j + 1) * L, t * L:(t + 1) * L] = m
            acc[t] = acc[t] + add_down(m.astype(F32))
    store = pltpu.make_async_copy(assign, assign_ref, local_sem.at[1])
    store.start()
    for t in range(col_tiles):
        cols_a[PASSES, nx + x, t:t + 1, :] = acc[t]
    first, middle, last = reduce_cols(PASSES)
    first()

    half = n_k // 2

    def rx1(first, n, side):
        k = first + 7
        return pltpu.make_async_remote_copy(
            src_ref=xfar.at[side, pl.ds(k, n)], dst_ref=xfar_in.at[side, pl.ds(k, n)],
            send_sem=rx1_send.at[side, k], recv_sem=rx1_recv.at[side, k],
            device_id=x_peer(1 if side == 0 else nx - 1), device_id_type=MESH)

    def rx2(first, n, side):
        k = first + 7
        return pltpu.make_async_remote_copy(
            src_ref=xsend.at[side, pl.ds(k, n)], dst_ref=xrecv.at[side, pl.ds(k, n)],
            send_sem=rx2_send.at[side, k], recv_sem=rx2_recv.at[side, k],
            device_id=x_peer(1 if side == 0 else nx - 1), device_id_type=MESH)

    def rz(e):
        return pltpu.make_async_remote_copy(
            src_ref=own.at[e + 7], dst_ref=zrecv.at[e + 7], send_sem=rz_send.at[e + 7], recv_sem=rz_recv.at[e + 7],
            device_id=z_peer(VIA[e] if e in VIA else STEP[e]), device_id_type=MESH)

    block = nx * chunk
    def products(first, n):
        depth_rows = pl.ds(pl.multiple_of(((z + nz + first) % nz) * block, block), n * block)
        k = first + 7

        def product(t, carry):
            where = pl.ds(pl.multiple_of(t * wide, wide), wide)
            part = jnp.dot(pts_t[depth_rows, :], assign[:, where], preferred_element_type=F32)
            prod[k:k + n, :, :, where] = part.reshape(n, nx, chunk, wide)
            return carry

        lax.fori_loop(0, tiles, product, 0)
        for e in range(first, first + n):
            far = prod[e + 7, (x + 2) % nx].astype(BF16)
            xfar[0, e + 7] = far[:, :half]
            xfar[1, e + 7] = far[:, half:]
        for side in range(2):
            rx1(first, n, side).start()

    def forward(first, n):
        for side in range(2):
            rx1(first, n, side).wait_recv()
        for side in range(2):
            for e in range(first, first + n):
                v = prod[e + 7, (x + 1 + 2 * side) % nx]
                w = xfar_in[side, e + 7].astype(F32)
                if side == 0:
                    xsend[side, e + 7, :, :half] = (v[:, :half] + w).astype(BF16)
                    xsend[side, e + 7, :, half:] = v[:, half:].astype(BF16)
                else:
                    xsend[side, e + 7, :, :half] = v[:, :half].astype(BF16)
                    xsend[side, e + 7, :, half:] = (v[:, half:] + w).astype(BF16)
            rx2(first, n, side).start()

    def centre(e):
        v = own[e + 7]
        for f in FEEDS[e]:
            rz(f).wait_recv()
            v = v + zrecv[f + 7]
        own[e + 7] = v
        rz(e).start()

    products(*PARTS[0])
    products(*PARTS[1])
    forward(*PARTS[0])
    products(*PARTS[2])
    forward(*PARTS[1])
    products(*PARTS[3])
    for i, (first, n) in enumerate(PARTS):
        for side in range(2):
            rx2(first, n, side).wait_recv()
        for e in range(first, first + n):
            own[e + 7] = prod[e + 7, x] + xrecv[0, e + 7].astype(F32) + xrecv[1, e + 7].astype(F32)
            if e in VIA:
                rz(e).start()
        if i + 2 < len(PARTS):
            forward(*PARTS[i + 2])
        if i == 0:
            products(*PARTS[4])
        if i:
            before = PARTS[i - 1]
            for e in FEEDS:
                if before[0] <= e < before[0] + before[1]:
                    centre(e)
        else:
            middle()
    counts = last()
    numer = own[7]
    for e in (1, -1, 3, -3):
        rz(e).wait_recv()
        numer = numer + zrecv[e + 7]
    for t in range(col_tiles):
        newc_ref[:, t * L:(t + 1) * L] = numer[:, t * L:(t + 1) * L] / counts[t:t + 1, :]
    for e in range(-7, 9):
        if e:
            rz(e).wait_send()
    for first, n in PARTS:
        for side in range(2):
            rx1(first, n, side).wait_send()
            rx2(first, n, side).wait_send()
    store.wait()


def on_device(nx, nz, nc, points, centroids_t):
    n_rows, n_d = points.shape
    chunk, n_k = centroids_t.shape
    rb, ct = n_rows // L, n_k // L
    assert nz == 16 and nx == 4
    vmem = pltpu.VMEM
    dma = pltpu.SemaphoreType.DMA
    return pl.pallas_call(
        functools.partial(kernel, nx, nz, nc),
        out_shape=(
            jax.ShapeDtypeStruct((chunk, n_k), F32),
            jax.ShapeDtypeStruct((n_rows, n_k), BF16),
        ),
        in_specs=[pl.BlockSpec(memory_space=pl.ANY), pl.BlockSpec(memory_space=vmem)],
        out_specs=(pl.BlockSpec(memory_space=vmem), pl.BlockSpec(memory_space=pl.ANY)),
        scratch_shapes=[
            vmem((n_rows, n_d), BF16),
            vmem((n_d + 3 * nx * chunk, n_rows), BF16),
            vmem((n_d, n_k), BF16),
            vmem((n_rows, n_k), F32),
            vmem((1, n_k), F32),
            vmem((n_rows, L), F32),
            vmem((n_rows, n_k), BF16),
            vmem((nz, chunk, n_k), F32),
            vmem((nz, nx, chunk, n_k), F32),
            vmem((2, nz, chunk, n_k // 2), BF16),
            vmem((2, nz, chunk, n_k // 2), BF16),
            vmem((2, nz, chunk, n_k), BF16),
            vmem((2, nz, chunk, n_k), BF16),
            vmem((nz, chunk, n_k), F32),
            vmem((nc, 2 * rb, L), F32),
            vmem((PASSES, nc, rb, L), F32),
            vmem((PASSES + 1, 4 * nx, ct, L), F32),
            vmem((PASSES + 1, len(CENTRES) + 1, ct, L), F32),
            dma((2,)),
            dma((nz, 3)), dma((nz, 3)),
            dma((nz,)), dma((nz,)),
            dma((1, nc)), dma((1, nc)),
            dma((PASSES, nc)), dma((PASSES, nc)),
            dma((PASSES + 1, 4 * nx)), dma((PASSES + 1, 4 * nx)),
            dma((PASSES + 1, len(CENTRES))), dma((PASSES + 1, len(CENTRES))),
            dma((2, nz)), dma((2, nz)),
            dma((2, nz)), dma((2, nz)),
            dma((nz,)), dma((nz,)),
        ],
        compiler_params=pltpu.CompilerParams(
            collective_id=0, has_side_effects=True, vmem_limit_bytes=50 * 1024 * 1024
        ),
    )(points, centroids_t)


def solution(mesh, nx=X_CHIPS):
    nz = mesh.shape["pts"] // nx
    return jax.shard_map(
        functools.partial(on_device, nx, nz, mesh.shape["cen"]),
        mesh=mesh,
        in_specs=(P("pts", None), P("pts", "cen")),
        out_specs=(P("pts", "cen"), P("pts", "cen")),
        check_vma=False,
    )
```

```python
import functools

import jax
import jax.numpy as jnp
from jax import lax
from jax.experimental import pallas as pl
from jax.experimental.pallas import tpu as pltpu
from jax.sharding import PartitionSpec as P

PASSES = 3
MESH = pl.DeviceIdType.MESH
L = 128
F32 = jnp.float32
BF16 = jnp.bfloat16
X_CHIPS = 4
VIA = {1: 1, -1: -1, 2: -1, 4: 1, 5: -1, 7: 1, 8: 2, -2: 1, -4: -1, -5: 1, -7: -1}
FEEDS = {6: (7, 5, 8), -6: (-7, -5), 3: (4, 2, 6), -3: (-4, -2, -6)}
STEP = {6: 3, -6: -3, 3: 3, -3: -3}
GREET_Z = (1, -1, 2, -2, 3, -3)
CENTRES = (6, -6, 3, -3)
PARTS = ((5, 4), (-7, 3), (2, 3), (-4, 3), (-1, 3))


def kernel(nx, nz, nc, points_ref, cent_ref, newc_ref, assign_ref,
           pts, pts_t, piece, mass, norms, top, assign, own, prod, xfar, xfar_in, xsend, xrecv, zrecv,
           soft, rows, cols_a, cols_b,
           local_sem, gx_send, gx_recv, gz_send, gz_recv, soft_send, soft_recv,
           row_send, row_recv, ca_send, ca_recv, cb_send, cb_recv,
           rx1_send, rx1_recv, rx2_send, rx2_recv, rz_send, rz_recv):
    n_rows, n_d = points_ref.shape
    chunk, n_k = cent_ref.shape
    row_blocks = n_rows // L
    col_tiles = n_k // L
    wide = min(256, n_k)

    p = lax.axis_index("pts")
    c = lax.axis_index("cen")
    z = p // nx
    x = p % nx

    def cen_peer(o):
        return {"cen": (c + o) % nc}

    def x_peer(o):
        return {"pts": z * nx + (x + o) % nx}

    def z_peer(o):
        return {"pts": ((z + nz + o) % nz) * nx + x}

    load = pltpu.make_async_copy(points_ref, pts, local_sem.at[0])
    load.start()
    load_c = pltpu.make_async_copy(
        cent_ref, piece.at[pl.ds(pl.multiple_of(p * chunk, chunk), chunk), :], local_sem.at[2])
    load_c.start()

    barrier = pltpu.get_barrier_semaphore()

    def greet(peer, n):
        def body(o, carry):
            pl.semaphore_signal(barrier, inc=1, device_id=peer(o), device_id_type=MESH)
            return carry
        lax.fori_loop(1, n, body, 0)

    greet(cen_peer, nc)
    greet(x_peer, nx)
    for e in GREET_Z:
        pl.semaphore_signal(barrier, inc=1, device_id=z_peer(e), device_id_type=MESH)
    pl.semaphore_wait(barrier, (nc - 1) + (nx - 1) + len(GREET_Z))

    def slab(e, side):
        first = ((z + nz + e) % nz) * nx + (x + nx + side) % nx
        return piece.at[pl.ds(pl.multiple_of(first * chunk, chunk), chunk), :]


    def gz(e, root):
        at = root - e + 7
        at = at + nz if at < 0 else at - nz if at >= nz else at
        part = slab(root, 0)
        return pltpu.make_async_remote_copy(
            src_ref=part, dst_ref=part, send_sem=gz_send.at[at], recv_sem=gz_recv.at[at],
            device_id=z_peer(e), device_id_type=MESH)

    def gz_got(e):
        part = slab(e, 0)
        return pltpu.make_async_remote_copy(
            src_ref=part, dst_ref=part, send_sem=gz_send.at[e + 7], recv_sem=gz_recv.at[e + 7],
            device_id=z_peer(1), device_id_type=MESH)

    def gx(e, frm, side):
        part = slab(e, frm)
        lane = 0 if frm == 0 and side == 1 else 1 if frm == 0 else 2
        return pltpu.make_async_remote_copy(
            src_ref=part, dst_ref=part, send_sem=gx_send.at[e + 7, lane], recv_sem=gx_recv.at[e + 7, lane],
            device_id=x_peer(nx + side), device_id_type=MESH)

    def gx_got(e, lane):
        part = slab(e, (-1, 1, 2)[lane])
        return pltpu.make_async_remote_copy(
            src_ref=part, dst_ref=part, send_sem=gx_send.at[e + 7, lane], recv_sem=gx_recv.at[e + 7, lane],
            device_id=x_peer(1), device_id_type=MESH)

    sent_z = []
    sent_x = []

    def go_z(e, root):
        gz(e, root).start()
        sent_z.append((e, root))

    def go_x(e, frm, side):
        gx(e, frm, side).start()
        sent_x.append((e, frm, side))

    def x_near(e):
        go_x(e, 0, 1)
        go_x(e, 0, -1)

    def x_on(e):
        gx_got(e, 0).wait_recv()
        gx_got(e, 1).wait_recv()
        if e % 2 == 0:
            go_x(e, -1, 1)
        else:
            go_x(e, 1, -1)

    d_blocks = n_d // L

    def turn(b):
        block = pts[:, pl.ds(pl.multiple_of(b * L, L), L)].astype(F32)
        pts_t[pl.ds(pl.multiple_of(b * L, L), L), :] = block.T.astype(BF16)

    def turns(first, last):
        def body(b, carry):
            turn(b)
            return carry
        lax.fori_loop(first, last, body, 0)

    load_c.wait()
    for e in (3, -3, 1, -1):
        go_z(e, 0)
    x_near(0)
    load.wait()
    turns(0, d_blocks // 2)
    for e in (1, -1):
        gz_got(e).wait_recv()
        x_near(e)
    for e in (3, -3):
        gz_got(e).wait_recv()
        go_z(-e, e)
        go_z(1, e)
        go_z(-1, e)
        x_near(e)
    x_on(0)
    x_on(1)
    x_on(-1)
    for e in (2, -2, 4, -4):
        gz_got(e).wait_recv()
        x_near(e)
    for e in (6, -6):
        gz_got(e).wait_recv()
        go_z(1, e)
        go_z(-1, e)
        if e == -6:
            go_z(2, e)
        x_near(e)
    for e in (3, -3, 2, -2, 4, -4):
        x_on(e)
    for e in (5, -5, 7, -7, 8):
        gz_got(e).wait_recv()
        x_near(e)
    turns(d_blocks // 2, d_blocks)
    ahead = 3 * nx * chunk
    pts_t[n_d:n_d + ahead, :] = pts_t[:ahead, :]
    x_on(6)
    x_on(-6)

    quarter = n_d // 4
    mine = z // (nz // 4)

    def depth(g):
        return pl.ds(pl.multiple_of(g * quarter, quarter), quarter)

    def dots_of(g, where):
        part = piece[depth(g), where]
        long = part.astype(F32)
        dots = jnp.dot(pts[:, depth(g)], part, preferred_element_type=F32)
        return dots, jnp.sum(long * long, axis=0, keepdims=True)

    def first_dots(t, carry):
        where = pl.ds(pl.multiple_of(t * wide, wide), wide)
        dots, squares = dots_of(mine, where)
        mass[:, where] = dots
        norms[:, where] = squares
        return carry

    def more_dots(g):
        def body(t, carry):
            where = pl.ds(pl.multiple_of(t * wide, wide), wide)
            dots, squares = dots_of(g, where)
            mass[:, where] += dots
            norms[:, where] += squares
            return carry
        return body

    tiles = n_k // wide
    for e in (0, 1, -1, 3, -3, 2, -2):
        gx_got(e, 2).wait_recv()
    lax.fori_loop(0, tiles, first_dots, 0)
    for e in (5, -5, 7, -7, 8):
        x_on(e)
    for e in (6, -6, 4, -4, 5, -5, 7, -7):
        gx_got(e, 2).wait_recv()
    lax.fori_loop(0, tiles, more_dots((mine + 1) % 4), 0)
    lax.fori_loop(0, tiles, more_dots((mine + 3) % 4), 0)
    gx_got(8, 2).wait_recv()
    top[...] = jnp.full(top.shape, -jnp.inf, F32)

    def logits(t, carry):
        where = pl.ds(pl.multiple_of(t * wide, wide), wide)
        dots, squares = dots_of((mine + 2) % 4, where)
        score = (2.0 * (mass[:, where] + dots) - (norms[:, where] + squares)) * 1.25
        mass[:, where] = score
        best = score[:, :L]
        for i in range(1, wide // L):
            best = jnp.maximum(best, score[:, i * L:(i + 1) * L])
        top[...] = jnp.maximum(top[...], best)
        return carry

    lax.fori_loop(0, tiles, logits, 0)

    for e, root in sent_z:
        gz(e, root).wait_send()
    for e, frm, side in sent_x:
        gx(e, frm, side).wait_send()

    def swap(buf, slot, n, me, peer, send, recv):
        def copy(o):
            return pltpu.make_async_remote_copy(
                src_ref=buf.at[me], dst_ref=buf.at[me], send_sem=send.at[slot, o],
                recv_sem=recv.at[slot, o], device_id=peer(o), device_id_type=MESH)

        def start(o, carry):
            copy(o).start()
            return carry

        def wait(o, carry):
            copy(o).wait()
            return carry

        return (lambda: lax.fori_loop(1, n, start, 0)), (lambda: lax.fori_loop(1, n, wait, 0))

    def total(buf, n):
        out = buf[0]
        for i in range(1, n):
            out = out + buf[i]
        return out

    def row_block(j):
        return pl.ds(pl.multiple_of(j * L, L), L)

    def weigh(j, carry):
        block = top[row_block(j), :]
        peak = jnp.max(block, axis=1, keepdims=True)
        soft[c, pl.ds(j, 1), :] = jnp.max(block.T, axis=0, keepdims=True)
        acc = jnp.zeros((L, L), F32)
        for t in range(col_tiles):
            w = jnp.exp(mass[row_block(j), t * L:(t + 1) * L] - peak)
            mass[row_block(j), t * L:(t + 1) * L] = w
            acc = acc + w
        soft[c, pl.ds(row_blocks + j, 1), :] = jnp.sum(acc.T, axis=0, keepdims=True)
        return carry

    lax.fori_loop(0, row_blocks, weigh, 0)
    start, wait = swap(soft, 0, nc, c, cen_peer, soft_send, soft_recv)
    start()
    wait()
    peaks = soft[0, :row_blocks]
    for i in range(1, nc):
        peaks = jnp.maximum(peaks, soft[i, :row_blocks])
    sums = jnp.zeros_like(peaks)
    for i in range(nc):
        sums = sums + soft[i, row_blocks:] * jnp.exp(soft[i, :row_blocks] - peaks)
    scale_rows = jnp.exp(soft[c, :row_blocks] - peaks) / sums

    def spread(scales, j):
        return jnp.broadcast_to(scales[j:j + 1, :], (L, L)).T

    def add_down(v):
        return jnp.sum(v, axis=0, keepdims=True)

    near = [(d, o) for d in (1, -1, 0) for o in range(nx) if d or o]
    opposite = [(8, o) for o in range(nx)]

    def col_copy(slot, d, o):
        lane = (1 - d) * nx + o if d != 8 else 3 * nx + o
        there = (1 - d) * nx + x if d != 8 else 3 * nx + x
        return pltpu.make_async_remote_copy(
            src_ref=cols_a.at[slot, nx + x], dst_ref=cols_a.at[slot, there],
            send_sem=ca_send.at[slot, lane], recv_sem=ca_recv.at[slot, lane],
            device_id={"pts": ((z + nz + d) % nz) * nx + (x + o) % nx}, device_id_type=MESH)

    def centre_copy(slot, i, e):
        return pltpu.make_async_remote_copy(
            src_ref=cols_b.at[slot, 0], dst_ref=cols_b.at[slot, 1 + i],
            send_sem=cb_send.at[slot, i], recv_sem=cb_recv.at[slot, i],
            device_id=z_peer(e), device_id_type=MESH)

    def reduce_cols(slot):
        def first():
            for d, o in opposite + near:
                col_copy(slot, d, o).start()

        def middle():
            for d, o in near:
                col_copy(slot, d, o).wait_recv()
            cols_b[slot, 0] = total(cols_a.at[slot], 3 * nx)
            for i, e in enumerate(CENTRES):
                centre_copy(slot, i, e).start()

        def last():
            for d, o in opposite:
                col_copy(slot, d, o).wait_recv()
            out = cols_a[slot, 3 * nx]
            for i in range(1, nx):
                out = out + cols_a[slot, 3 * nx + i]
            for i, e in enumerate(CENTRES):
                centre_copy(slot, i, e).wait_recv()
            for i in range(len(CENTRES) + 1):
                out = out + cols_b[slot, i]
            for i, e in enumerate(CENTRES):
                centre_copy(slot, i, e).wait_send()
            for d, o in opposite + near:
                col_copy(slot, d, o).wait_send()
            return out

        return first, middle, last

    for turn_no in range(PASSES):
        acc = [jnp.zeros((1, L), F32) for _ in range(col_tiles)]
        for j in range(row_blocks):
            scale = spread(scale_rows, j)
            for t in range(col_tiles):
                m = mass[j * L:(j + 1) * L, t * L:(t + 1) * L] * scale
                mass[j * L:(j + 1) * L, t * L:(t + 1) * L] = m
                acc[t] = acc[t] + add_down(m)
        for t in range(col_tiles):
            cols_a[turn_no, nx + x, t:t + 1, :] = acc[t]
        first, middle, last = reduce_cols(turn_no)
        first()
        middle()
        scale_cols = 1.0 / last()
        for j in range(row_blocks):
            acc_r = jnp.zeros((L, L), F32)
            for t in range(col_tiles):
                m = mass[j * L:(j + 1) * L, t * L:(t + 1) * L] * scale_cols[t:t + 1, :]
                mass[j * L:(j + 1) * L, t * L:(t + 1) * L] = m
                acc_r = acc_r + m
            rows[turn_no, c, j:j + 1, :] = add_down(acc_r.T)
        start, wait = swap(rows.at[turn_no], turn_no, nc, c, cen_peer, row_send, row_recv)
        start()
        wait()
        scale_rows = 1.0 / total(rows.at[turn_no], nc)

    acc = [jnp.zeros((1, L), F32) for _ in range(col_tiles)]
    for j in range(row_blocks):
        scale = spread(scale_rows, j)
        for t in range(col_tiles):
            m = (mass[j * L:(j + 1) * L, t * L:(t + 1) * L] * scale).astype(BF16)
            assign[j * L:(j + 1) * L, t * L:(t + 1) * L] = m
            acc[t] = acc[t] + add_down(m.astype(F32))
    store = pltpu.make_async_copy(assign, assign_ref, local_sem.at[1])
    store.start()
    for t in range(col_tiles):
        cols_a[PASSES, nx + x, t:t + 1, :] = acc[t]
    first, middle, last = reduce_cols(PASSES)
    first()

    half = n_k // 2

    def rx1(first, n, side):
        k = first + 7
        return pltpu.make_async_remote_copy(
            src_ref=xfar.at[side, pl.ds(k, n)], dst_ref=xfar_in.at[side, pl.ds(k, n)],
            send_sem=rx1_send.at[side, k], recv_sem=rx1_recv.at[side, k],
            device_id=x_peer(1 if side == 0 else nx - 1), device_id_type=MESH)

    def rx2(first, n, side):
        k = first + 7
        return pltpu.make_async_remote_copy(
            src_ref=xsend.at[side, pl.ds(k, n)], dst_ref=xrecv.at[side, pl.ds(k, n)],
            send_sem=rx2_send.at[side, k], recv_sem=rx2_recv.at[side, k],
            device_id=x_peer(1 if side == 0 else nx - 1), device_id_type=MESH)

    def rz(f, h):
        to = VIA[f] if f in VIA else STEP[f]
        return pltpu.make_async_remote_copy(
            src_ref=own.at[h, f + 7], dst_ref=zrecv.at[h, f + 7],
            send_sem=rz_send.at[h, f + 7], recv_sem=rz_recv.at[h, f + 7],
            device_id=z_peer(-to if h else to), device_id_type=MESH)

    block = nx * chunk
    narrow = min(wide, half)

    def products(first, n):
        k = first + 7
        for h in range(2):
            lowest = 1 - first - n if h else first
            depth_rows = pl.ds(pl.multiple_of(((z + nz + lowest) % nz) * block, block), n * block)

            def product(t, carry):
                where = pl.ds(pl.multiple_of(h * half + t * narrow, narrow), narrow)
                part = jnp.dot(pts_t[depth_rows, :], assign[:, where], preferred_element_type=F32)
                part = part.reshape(n, nx, chunk, narrow)
                for i in range(n):
                    prod[k + (n - 1 - i if h else i), :, :, where] = part[i]
                return carry

            lax.fori_loop(0, half // narrow, product, 0)
        for e in range(first, first + n):
            far = prod[e + 7, (x + 2) % nx].astype(BF16)
            xfar[0, e + 7] = far[:, :half]
            xfar[1, e + 7] = far[:, half:]
        for side in range(2):
            rx1(first, n, side).start()

    def forward(first, n):
        for side in range(2):
            rx1(first, n, side).wait_recv()
        for side in range(2):
            for e in range(first, first + n):
                v = prod[e + 7, (x + 1 + 2 * side) % nx]
                w = xfar_in[side, e + 7].astype(F32)
                if side == 0:
                    xsend[side, e + 7, :, :half] = (v[:, :half] + w).astype(BF16)
                    xsend[side, e + 7, :, half:] = v[:, half:].astype(BF16)
                else:
                    xsend[side, e + 7, :, :half] = v[:, :half].astype(BF16)
                    xsend[side, e + 7, :, half:] = (v[:, half:] + w).astype(BF16)
            rx2(first, n, side).start()

    def centre(f):
        for h in range(2):
            v = own[h, f + 7]
            for g in FEEDS[f]:
                rz(g, h).wait_recv()
                v = v + zrecv[h, g + 7]
            own[h, f + 7] = v
            rz(f, h).start()

    products(*PARTS[0])
    products(*PARTS[1])
    forward(*PARTS[0])
    products(*PARTS[2])
    forward(*PARTS[1])
    products(*PARTS[3])
    for i, (first, n) in enumerate(PARTS):
        for side in range(2):
            rx2(first, n, side).wait_recv()
        for e in range(first, first + n):
            v = prod[e + 7, x] + xrecv[0, e + 7].astype(F32) + xrecv[1, e + 7].astype(F32)
            for h in range(2):
                own[h, e + 7] = v[:, h * half:(h + 1) * half]
                if e in VIA:
                    rz(e, h).start()
        if i + 2 < len(PARTS):
            forward(*PARTS[i + 2])
        if i == 0:
            products(*PARTS[4])
        if i:
            before = PARTS[i - 1]
            for e in FEEDS:
                if before[0] <= e < before[0] + before[1]:
                    centre(e)
        else:
            middle()
    counts = last()
    for h in range(2):
        numer = own[h, 7]
        for f in (1, -1, 3, -3):
            rz(f, h).wait_recv()
            numer = numer + zrecv[h, f + 7]
        for t in range(col_tiles // 2):
            u = h * (col_tiles // 2) + t
            newc_ref[:, u * L:(u + 1) * L] = numer[:, t * L:(t + 1) * L] / counts[u:u + 1, :]
    for h in range(2):
        for f in range(-7, 9):
            if f:
                rz(f, h).wait_send()
    for first, n in PARTS:
        for side in range(2):
            rx1(first, n, side).wait_send()
            rx2(first, n, side).wait_send()
    store.wait()


def on_device(nx, nz, nc, points, centroids_t):
    n_rows, n_d = points.shape
    chunk, n_k = centroids_t.shape
    rb, ct = n_rows // L, n_k // L
    assert nz == 16 and nx == 4
    vmem = pltpu.VMEM
    dma = pltpu.SemaphoreType.DMA
    return pl.pallas_call(
        functools.partial(kernel, nx, nz, nc),
        out_shape=(
            jax.ShapeDtypeStruct((chunk, n_k), F32),
            jax.ShapeDtypeStruct((n_rows, n_k), BF16),
        ),
        in_specs=[pl.BlockSpec(memory_space=pltpu.HBM), pl.BlockSpec(memory_space=pltpu.HBM)],
        out_specs=(pl.BlockSpec(memory_space=vmem), pl.BlockSpec(memory_space=pl.ANY)),
        scratch_shapes=[
            vmem((n_rows, n_d), BF16),
            vmem((n_d + 3 * nx * chunk, n_rows), BF16),
            vmem((n_d, n_k), BF16),
            vmem((n_rows, n_k), F32),
            vmem((1, n_k), F32),
            vmem((n_rows, L), F32),
            vmem((n_rows, n_k), BF16),
            vmem((2, nz, chunk, n_k // 2), F32),
            vmem((nz, nx, chunk, n_k), F32),
            vmem((2, nz, chunk, n_k // 2), BF16),
            vmem((2, nz, chunk, n_k // 2), BF16),
            vmem((2, nz, chunk, n_k), BF16),
            vmem((2, nz, chunk, n_k), BF16),
            vmem((2, nz, chunk, n_k // 2), F32),
            vmem((nc, 2 * rb, L), F32),
            vmem((PASSES, nc, rb, L), F32),
            vmem((PASSES + 1, 4 * nx, ct, L), F32),
            vmem((PASSES + 1, len(CENTRES) + 1, ct, L), F32),
            dma((3,)),
            dma((nz, 3)), dma((nz, 3)),
            dma((nz,)), dma((nz,)),
            dma((1, nc)), dma((1, nc)),
            dma((PASSES, nc)), dma((PASSES, nc)),
            dma((PASSES + 1, 4 * nx)), dma((PASSES + 1, 4 * nx)),
            dma((PASSES + 1, len(CENTRES))), dma((PASSES + 1, len(CENTRES))),
            dma((2, nz)), dma((2, nz)),
            dma((2, nz)), dma((2, nz)),
            dma((2, nz)), dma((2, nz)),
        ],
        compiler_params=pltpu.CompilerParams(
            collective_id=0, has_side_effects=True, vmem_limit_bytes=50 * 1024 * 1024
        ),
    )(points, centroids_t)


def solution(mesh, nx=X_CHIPS):
    nz = mesh.shape["pts"] // nx
    return jax.shard_map(
        functools.partial(on_device, nx, nz, mesh.shape["cen"]),
        mesh=mesh,
        in_specs=(P("pts", None), P("pts", "cen")),
        out_specs=(P("pts", "cen"), P("pts", "cen")),
        check_vma=False,
    )
```

```python
import functools

import jax
import jax.numpy as jnp
from jax import lax
from jax.experimental import pallas as pl
from jax.experimental.pallas import tpu as pltpu
from jax.sharding import PartitionSpec as P

PASSES = 3
MESH = pl.DeviceIdType.MESH
L = 128
F32 = jnp.float32
BF16 = jnp.bfloat16
X_CHIPS = 4
VIA = {1: 1, -1: -1, 2: -1, 4: 1, 5: -1, 7: 1, 8: 2, -2: 1, -4: -1, -5: 1, -7: -1}
FEEDS = {6: (7, 5, 8), -6: (-7, -5), 3: (4, 2, 6), -3: (-4, -2, -6)}
STEP = {6: 3, -6: -3, 3: 3, -3: -3}
GREET_Z = (1, -1, 2, -2, 3, -3)
CENTRES = (6, -6, 3, -3)
PARTS = ((7, 2), (5, 2), (-7, 3), (2, 3), (-4, 3), (-1, 3))


def kernel(nx, nz, nc, points_ref, cent_ref, newc_ref, assign_ref,
           pts, pts_t, piece, mass, norms, top, assign, own, prod, xfar, xfar_in, xsend, xrecv, zrecv,
           soft, rows, cols_a, cols_b,
           local_sem, gx_send, gx_recv, gz_send, gz_recv, soft_send, soft_recv,
           row_send, row_recv, ca_send, ca_recv, cb_send, cb_recv,
           rx1_send, rx1_recv, rx2_send, rx2_recv, rz_send, rz_recv):
    n_rows, n_d = points_ref.shape
    chunk, n_k = cent_ref.shape
    row_blocks = n_rows // L
    col_tiles = n_k // L
    wide = min(512, n_k)

    p = lax.axis_index("pts")
    c = lax.axis_index("cen")
    z = p // nx
    x = p % nx

    def cen_peer(o):
        return {"cen": (c + o) % nc}

    def x_peer(o):
        return {"pts": z * nx + (x + o) % nx}

    def z_peer(o):
        return {"pts": ((z + nz + o) % nz) * nx + x}

    load = pltpu.make_async_copy(points_ref, pts, local_sem.at[0])
    load.start()
    load_c = pltpu.make_async_copy(
        cent_ref, piece.at[pl.ds(pl.multiple_of(p * chunk, chunk), chunk), :], local_sem.at[2])
    load_c.start()

    barrier = pltpu.get_barrier_semaphore()

    def greet(peer, n):
        def body(o, carry):
            pl.semaphore_signal(barrier, inc=1, device_id=peer(o), device_id_type=MESH)
            return carry
        lax.fori_loop(1, n, body, 0)

    greet(cen_peer, nc)
    greet(x_peer, nx)
    for e in GREET_Z:
        pl.semaphore_signal(barrier, inc=1, device_id=z_peer(e), device_id_type=MESH)
    pl.semaphore_wait(barrier, (nc - 1) + (nx - 1) + len(GREET_Z))

    def slab(e, side):
        first = ((z + nz + e) % nz) * nx + (x + nx + side) % nx
        return piece.at[pl.ds(pl.multiple_of(first * chunk, chunk), chunk), :]


    def gz(e, root):
        at = root - e + 7
        at = at + nz if at < 0 else at - nz if at >= nz else at
        part = slab(root, 0)
        return pltpu.make_async_remote_copy(
            src_ref=part, dst_ref=part, send_sem=gz_send.at[at], recv_sem=gz_recv.at[at],
            device_id=z_peer(e), device_id_type=MESH)

    def gz_got(e):
        part = slab(e, 0)
        return pltpu.make_async_remote_copy(
            src_ref=part, dst_ref=part, send_sem=gz_send.at[e + 7], recv_sem=gz_recv.at[e + 7],
            device_id=z_peer(1), device_id_type=MESH)

    def gx(e, frm, side):
        part = slab(e, frm)
        lane = 0 if frm == 0 and side == 1 else 1 if frm == 0 else 2
        return pltpu.make_async_remote_copy(
            src_ref=part, dst_ref=part, send_sem=gx_send.at[e + 7, lane], recv_sem=gx_recv.at[e + 7, lane],
            device_id=x_peer(nx + side), device_id_type=MESH)

    def gx_got(e, lane):
        part = slab(e, (-1, 1, 2)[lane])
        return pltpu.make_async_remote_copy(
            src_ref=part, dst_ref=part, send_sem=gx_send.at[e + 7, lane], recv_sem=gx_recv.at[e + 7, lane],
            device_id=x_peer(1), device_id_type=MESH)

    sent_z = []
    sent_x = []

    def go_z(e, root):
        gz(e, root).start()
        sent_z.append((e, root))

    def go_x(e, frm, side):
        gx(e, frm, side).start()
        sent_x.append((e, frm, side))

    def x_near(e):
        go_x(e, 0, 1)
        go_x(e, 0, -1)

    def x_on(e):
        gx_got(e, 0).wait_recv()
        gx_got(e, 1).wait_recv()
        if e % 2 == 0:
            go_x(e, -1, 1)
        else:
            go_x(e, 1, -1)

    d_blocks = n_d // L

    def turn(b):
        block = pts[:, pl.ds(pl.multiple_of(b * L, L), L)].astype(F32)
        pts_t[pl.ds(pl.multiple_of(b * L, L), L), :] = block.T.astype(BF16)

    def turns(first, last):
        def body(b, carry):
            turn(b)
            return carry
        lax.fori_loop(first, last, body, 0)

    load_c.wait()
    for e in (3, -3, 1, -1):
        go_z(e, 0)
    x_near(0)
    load.wait()
    turns(0, d_blocks // 2)
    for e in (1, -1):
        gz_got(e).wait_recv()
        x_near(e)
    for e in (3, -3):
        gz_got(e).wait_recv()
        go_z(-e, e)
        go_z(1, e)
        go_z(-1, e)
        x_near(e)
    x_on(0)
    x_on(1)
    x_on(-1)
    for e in (2, -2, 4, -4):
        gz_got(e).wait_recv()
        x_near(e)
    for e in (6, -6):
        gz_got(e).wait_recv()
        go_z(1, e)
        go_z(-1, e)
        if e == -6:
            go_z(2, e)
        x_near(e)
    for e in (3, -3, 2, -2, 4, -4):
        x_on(e)
    for e in (5, -5, 7, -7, 8):
        gz_got(e).wait_recv()
        x_near(e)
    turns(d_blocks // 2, d_blocks)
    ahead = 3 * nx * chunk
    pts_t[n_d:n_d + ahead, :] = pts_t[:ahead, :]
    x_on(6)
    x_on(-6)

    quarter = n_d // 4
    mine = z // (nz // 4)

    def depth(g):
        return pl.ds(pl.multiple_of(g * quarter, quarter), quarter)

    def dots_of(g, where):
        part = piece[depth(g), where]
        long = part.astype(F32)
        dots = jnp.dot(pts[:, depth(g)], part, preferred_element_type=F32)
        return dots, jnp.sum(long * long, axis=0, keepdims=True)

    def first_dots(t, carry):
        where = pl.ds(pl.multiple_of(t * wide, wide), wide)
        dots, squares = dots_of(mine, where)
        mass[:, where] = dots
        norms[:, where] = squares
        return carry

    def more_dots(g):
        def body(t, carry):
            where = pl.ds(pl.multiple_of(t * wide, wide), wide)
            dots, squares = dots_of(g, where)
            mass[:, where] += dots
            norms[:, where] += squares
            return carry
        return body

    tiles = n_k // wide
    for e in (0, 1, -1, 3, -3, 2, -2):
        gx_got(e, 2).wait_recv()
    lax.fori_loop(0, tiles, first_dots, 0)
    for e in (5, -5, 7, -7, 8):
        x_on(e)
    for e in (6, -6, 4, -4, 5, -5, 7, -7):
        gx_got(e, 2).wait_recv()
    lax.fori_loop(0, tiles, more_dots((mine + 1) % 4), 0)
    lax.fori_loop(0, tiles, more_dots((mine + 3) % 4), 0)
    gx_got(8, 2).wait_recv()
    top[...] = jnp.full(top.shape, -jnp.inf, F32)

    def logits(t, carry):
        where = pl.ds(pl.multiple_of(t * wide, wide), wide)
        dots, squares = dots_of((mine + 2) % 4, where)
        score = (2.0 * (mass[:, where] + dots) - (norms[:, where] + squares)) * 1.25
        mass[:, where] = score
        best = score[:, :L]
        for i in range(1, wide // L):
            best = jnp.maximum(best, score[:, i * L:(i + 1) * L])
        top[...] = jnp.maximum(top[...], best)
        return carry

    lax.fori_loop(0, tiles, logits, 0)

    for e, root in sent_z:
        gz(e, root).wait_send()
    for e, frm, side in sent_x:
        gx(e, frm, side).wait_send()

    def swap(buf, slot, n, me, peer, send, recv):
        def copy(o):
            return pltpu.make_async_remote_copy(
                src_ref=buf.at[me], dst_ref=buf.at[me], send_sem=send.at[slot, o],
                recv_sem=recv.at[slot, o], device_id=peer(o), device_id_type=MESH)

        def start():
            for o in sorted(range(1, n), key=lambda o: abs(o - n // 2)):
                copy(o).start()

        def wait():
            for o in range(1, n):
                copy(o).wait_recv()
            for o in range(1, n):
                copy(o).wait_send()

        return start, wait

    def total(buf, n):
        out = buf[0]
        for i in range(1, n):
            out = out + buf[i]
        return out

    def row_block(j):
        return pl.ds(pl.multiple_of(j * L, L), L)

    def weigh(j, carry):
        block = top[row_block(j), :]
        peak = jnp.max(block, axis=1, keepdims=True)
        soft[c, pl.ds(j, 1), :] = jnp.max(block.T, axis=0, keepdims=True)
        acc = jnp.zeros((L, L), F32)
        for t in range(col_tiles):
            w = jnp.exp(mass[row_block(j), t * L:(t + 1) * L] - peak)
            mass[row_block(j), t * L:(t + 1) * L] = w
            acc = acc + w
        soft[c, pl.ds(row_blocks + j, 1), :] = jnp.sum(acc.T, axis=0, keepdims=True)
        return carry

    lax.fori_loop(0, row_blocks, weigh, 0)
    start, wait = swap(soft, 0, nc, c, cen_peer, soft_send, soft_recv)
    start()
    wait()
    peaks = soft[0, :row_blocks]
    for i in range(1, nc):
        peaks = jnp.maximum(peaks, soft[i, :row_blocks])
    sums = jnp.zeros_like(peaks)
    for i in range(nc):
        sums = sums + soft[i, row_blocks:] * jnp.exp(soft[i, :row_blocks] - peaks)
    scale_rows = jnp.exp(soft[c, :row_blocks] - peaks) / sums

    def spread(scales, j):
        return jnp.broadcast_to(scales[j:j + 1, :], (L, L)).T

    def add_down(v):
        return jnp.sum(v, axis=0, keepdims=True)

    near = [(d, o) for d in (1, -1, 0) for o in range(nx) if d or o]
    opposite = [(8, o) for o in range(nx)]

    def col_copy(slot, d, o):
        lane = (1 - d) * nx + o if d != 8 else 3 * nx + o
        there = (1 - d) * nx + x if d != 8 else 3 * nx + x
        return pltpu.make_async_remote_copy(
            src_ref=cols_a.at[slot, nx + x], dst_ref=cols_a.at[slot, there],
            send_sem=ca_send.at[slot, lane], recv_sem=ca_recv.at[slot, lane],
            device_id={"pts": ((z + nz + d) % nz) * nx + (x + o) % nx}, device_id_type=MESH)

    def centre_copy(slot, i, e):
        return pltpu.make_async_remote_copy(
            src_ref=cols_b.at[slot, 0], dst_ref=cols_b.at[slot, 1 + i],
            send_sem=cb_send.at[slot, i], recv_sem=cb_recv.at[slot, i],
            device_id=z_peer(e), device_id_type=MESH)

    def reduce_cols(slot):
        def first():
            for d, o in opposite + near:
                col_copy(slot, d, o).start()

        def middle():
            for d, o in near:
                col_copy(slot, d, o).wait_recv()
            cols_b[slot, 0] = total(cols_a.at[slot], 3 * nx)
            for i, e in enumerate(CENTRES):
                centre_copy(slot, i, e).start()

        def last():
            for d, o in opposite:
                col_copy(slot, d, o).wait_recv()
            out = cols_a[slot, 3 * nx]
            for i in range(1, nx):
                out = out + cols_a[slot, 3 * nx + i]
            for i, e in enumerate(CENTRES):
                centre_copy(slot, i, e).wait_recv()
            for i in range(len(CENTRES) + 1):
                out = out + cols_b[slot, i]
            for i, e in enumerate(CENTRES):
                centre_copy(slot, i, e).wait_send()
            for d, o in opposite + near:
                col_copy(slot, d, o).wait_send()
            return out

        return first, middle, last

    for turn_no in range(PASSES):
        acc = [jnp.zeros((1, L), F32) for _ in range(col_tiles)]
        for j in range(row_blocks):
            scale = spread(scale_rows, j)
            for t in range(col_tiles):
                m = mass[j * L:(j + 1) * L, t * L:(t + 1) * L] * scale
                mass[j * L:(j + 1) * L, t * L:(t + 1) * L] = m
                acc[t] = acc[t] + add_down(m)
        for t in range(col_tiles):
            cols_a[turn_no, nx + x, t:t + 1, :] = acc[t]
        first, middle, last = reduce_cols(turn_no)
        first()
        middle()
        scale_cols = 1.0 / last()
        for j in range(row_blocks):
            acc_r = jnp.zeros((L, L), F32)
            for t in range(col_tiles):
                m = mass[j * L:(j + 1) * L, t * L:(t + 1) * L] * scale_cols[t:t + 1, :]
                mass[j * L:(j + 1) * L, t * L:(t + 1) * L] = m
                acc_r = acc_r + m
            rows[turn_no, c, j:j + 1, :] = add_down(acc_r.T)
        start, wait = swap(rows.at[turn_no], turn_no, nc, c, cen_peer, row_send, row_recv)
        start()
        wait()
        scale_rows = 1.0 / total(rows.at[turn_no], nc)

    acc = [jnp.zeros((1, L), F32) for _ in range(col_tiles)]
    for j in range(row_blocks):
        scale = spread(scale_rows, j)
        for t in range(col_tiles):
            m = (mass[j * L:(j + 1) * L, t * L:(t + 1) * L] * scale).astype(BF16)
            assign[j * L:(j + 1) * L, t * L:(t + 1) * L] = m
            acc[t] = acc[t] + add_down(m.astype(F32))
    store = pltpu.make_async_copy(assign, assign_ref, local_sem.at[1])
    store.start()
    for t in range(col_tiles):
        cols_a[PASSES, nx + x, t:t + 1, :] = acc[t]
    first, middle, last = reduce_cols(PASSES)
    first()

    half = n_k // 2

    def rx1(first, n, side):
        k = first + 7
        return pltpu.make_async_remote_copy(
            src_ref=xfar.at[side, pl.ds(k, n)], dst_ref=xfar_in.at[side, pl.ds(k, n)],
            send_sem=rx1_send.at[side, k], recv_sem=rx1_recv.at[side, k],
            device_id=x_peer(1 if side == 0 else nx - 1), device_id_type=MESH)

    def rx2(first, n, side):
        k = first + 7
        return pltpu.make_async_remote_copy(
            src_ref=xsend.at[side, pl.ds(k, n)], dst_ref=xrecv.at[side, pl.ds(k, n)],
            send_sem=rx2_send.at[side, k], recv_sem=rx2_recv.at[side, k],
            device_id=x_peer(1 if side == 0 else nx - 1), device_id_type=MESH)

    def rz(f, h):
        to = VIA[f] if f in VIA else STEP[f]
        return pltpu.make_async_remote_copy(
            src_ref=own.at[h, f + 7], dst_ref=zrecv.at[h, f + 7],
            send_sem=rz_send.at[h, f + 7], recv_sem=rz_recv.at[h, f + 7],
            device_id=z_peer(-to if h else to), device_id_type=MESH)

    block = nx * chunk
    narrow = min(wide, half)

    def products(first, n):
        k = first + 7
        for h in range(2):
            lowest = 1 - first - n if h else first
            depth_rows = pl.ds(pl.multiple_of(((z + nz + lowest) % nz) * block, block), n * block)

            def product(t, carry):
                where = pl.ds(pl.multiple_of(h * half + t * narrow, narrow), narrow)
                part = jnp.dot(pts_t[depth_rows, :], assign[:, where], preferred_element_type=F32)
                part = part.reshape(n, nx, chunk, narrow)
                for i in range(n):
                    prod[k + (n - 1 - i if h else i), :, :, where] = part[i]
                return carry

            lax.fori_loop(0, half // narrow, product, 0)
        for e in range(first, first + n):
            far = prod[e + 7, (x + 2) % nx].astype(BF16)
            xfar[0, e + 7] = far[:, :half]
            xfar[1, e + 7] = far[:, half:]
        for side in range(2):
            rx1(first, n, side).start()

    def forward(first, n):
        for side in range(2):
            rx1(first, n, side).wait_recv()
        for side in range(2):
            for e in range(first, first + n):
                v = prod[e + 7, (x + 1 + 2 * side) % nx]
                w = xfar_in[side, e + 7].astype(F32)
                if side == 0:
                    xsend[side, e + 7, :, :half] = (v[:, :half] + w).astype(BF16)
                    xsend[side, e + 7, :, half:] = v[:, half:].astype(BF16)
                else:
                    xsend[side, e + 7, :, :half] = v[:, :half].astype(BF16)
                    xsend[side, e + 7, :, half:] = (v[:, half:] + w).astype(BF16)
            rx2(first, n, side).start()

    def centre(f):
        for h in range(2):
            v = own[h, f + 7]
            for g in FEEDS[f]:
                rz(g, h).wait_recv()
                v = v + zrecv[h, g + 7]
            own[h, f + 7] = v
            rz(f, h).start()

    products(*PARTS[0])
    products(*PARTS[1])
    forward(*PARTS[0])
    products(*PARTS[2])
    forward(*PARTS[1])
    products(*PARTS[3])
    for i, (first, n) in enumerate(PARTS):
        for side in range(2):
            rx2(first, n, side).wait_recv()
        for e in range(first, first + n):
            v = prod[e + 7, x] + xrecv[0, e + 7].astype(F32) + xrecv[1, e + 7].astype(F32)
            for h in range(2):
                own[h, e + 7] = v[:, h * half:(h + 1) * half]
                if e in VIA:
                    rz(e, h).start()
        if i + 2 < len(PARTS):
            forward(*PARTS[i + 2])
        if i < 2:
            products(*PARTS[4 + i])
        if i:
            before = PARTS[i - 1]
            for e in FEEDS:
                if before[0] <= e < before[0] + before[1]:
                    centre(e)
        else:
            middle()
    counts = last()
    for h in range(2):
        numer = own[h, 7]
        for f in (1, -1, 3, -3):
            rz(f, h).wait_recv()
            numer = numer + zrecv[h, f + 7]
        for t in range(col_tiles // 2):
            u = h * (col_tiles // 2) + t
            newc_ref[:, u * L:(u + 1) * L] = numer[:, t * L:(t + 1) * L] / counts[u:u + 1, :]
    for h in range(2):
        for f in range(-7, 9):
            if f:
                rz(f, h).wait_send()
    for first, n in PARTS:
        for side in range(2):
            rx1(first, n, side).wait_send()
            rx2(first, n, side).wait_send()
    store.wait()


def on_device(nx, nz, nc, points, centroids_t):
    n_rows, n_d = points.shape
    chunk, n_k = centroids_t.shape
    rb, ct = n_rows // L, n_k // L
    assert nz == 16 and nx == 4
    vmem = pltpu.VMEM
    dma = pltpu.SemaphoreType.DMA
    return pl.pallas_call(
        functools.partial(kernel, nx, nz, nc),
        out_shape=(
            jax.ShapeDtypeStruct((chunk, n_k), F32),
            jax.ShapeDtypeStruct((n_rows, n_k), BF16),
        ),
        in_specs=[pl.BlockSpec(memory_space=pltpu.HBM), pl.BlockSpec(memory_space=pltpu.HBM)],
        out_specs=(pl.BlockSpec(memory_space=vmem), pl.BlockSpec(memory_space=pl.ANY)),
        scratch_shapes=[
            vmem((n_rows, n_d), BF16),
            vmem((n_d + 3 * nx * chunk, n_rows), BF16),
            vmem((n_d, n_k), BF16),
            vmem((n_rows, n_k), F32),
            vmem((1, n_k), F32),
            vmem((n_rows, L), F32),
            vmem((n_rows, n_k), BF16),
            vmem((2, nz, chunk, n_k // 2), F32),
            vmem((nz, nx, chunk, n_k), F32),
            vmem((2, nz, chunk, n_k // 2), BF16),
            vmem((2, nz, chunk, n_k // 2), BF16),
            vmem((2, nz, chunk, n_k), BF16),
            vmem((2, nz, chunk, n_k), BF16),
            vmem((2, nz, chunk, n_k // 2), F32),
            vmem((nc, 2 * rb, L), F32),
            vmem((PASSES, nc, rb, L), F32),
            vmem((PASSES + 1, 4 * nx, ct, L), F32),
            vmem((PASSES + 1, len(CENTRES) + 1, ct, L), F32),
            dma((3,)),
            dma((nz, 3)), dma((nz, 3)),
            dma((nz,)), dma((nz,)),
            dma((1, nc)), dma((1, nc)),
            dma((PASSES, nc)), dma((PASSES, nc)),
            dma((PASSES + 1, 4 * nx)), dma((PASSES + 1, 4 * nx)),
            dma((PASSES + 1, len(CENTRES))), dma((PASSES + 1, len(CENTRES))),
            dma((2, nz)), dma((2, nz)),
            dma((2, nz)), dma((2, nz)),
            dma((2, nz)), dma((2, nz)),
        ],
        compiler_params=pltpu.CompilerParams(
            collective_id=0, has_side_effects=True, vmem_limit_bytes=50 * 1024 * 1024
        ),
    )(points, centroids_t)


def solution(mesh, nx=X_CHIPS):
    nz = mesh.shape["pts"] // nx
    return jax.shard_map(
        functools.partial(on_device, nx, nz, mesh.shape["cen"]),
        mesh=mesh,
        in_specs=(P("pts", None), P("pts", "cen")),
        out_specs=(P("pts", "cen"), P("pts", "cen")),
        check_vma=False,
    )
```
